512 devices in a mesh: gx: 16 (over x, y_lo, core), gy: 32 (over z, y_hi).
Axes of the slice: x: 4, y: 4 (y_hi: 2, y_lo: 2; y = y_hi * 2 + y_lo), z: 16, core: 2. Of those that a mesh axis runs over, the one named last changes fastest.
Arguments:
- volume: bfloat16 [2, 64, 512, 2048], P(None, None, 'gy', 'gx'), may hold values from -6 to 6
- pupil_phase: float32 [16, 512, 2048], P(None, 'gy', 'gx'), may hold values from -3.140625 to 3.140625
Outputs:
- decorrelation: float32 [16, 512, 2048], P(None, 'gy', 'gx')
The draws below stay inside these ranges and needn't reach their ends.
All inputs are finite; a program needn't handle non-finite values.
Results may differ from the reference program's by a relative error of at most 0.0075.
Values may be sent and summed in bfloat16 or wider, within the bound.
A program may use at most 64 MiB of HBM per device.

```python
import math
import jax
import jax.numpy as jnp
from jax import lax

R = 4
Z = 16
LOW = 128
S = 64
NX = 2048
NY = 512


def draw_volume(key, part):
    key = jax.random.fold_in(key, 7)
    subkeys = jax.random.split(key, 3)
    flow_map = jnp.exp(jax.random.uniform(subkeys[2], (1, 1, Z, NY, NX), jnp.float32, math.log(0.05), math.log(3.0)))
    static = jnp.clip(jax.random.normal(subkeys[0], (2, 1, Z, NY, NX), jnp.float32), -4.0, 4.0)
    noise_part = jnp.clip(jax.random.normal(subkeys[1], (2, R, Z, NY, NX), jnp.float32), -4.0, 4.0)
    values = (static + flow_map * noise_part) / jnp.sqrt(1.0 + flow_map * flow_map)
    return values.reshape(2, R * Z, NY, NX).astype(jnp.bfloat16)


def setup_inputs(seed: int = 0) -> dict:
    seeds = jax.random.split(jax.random.key(seed), 3)
    return {
        "volume": draw_volume(jax.random.fold_in(seeds[2], 71), 0),
        "pupil_phase": jnp.clip(jax.random.uniform(seeds[1], (Z, NY, NX), jnp.float32, -3.140625, 3.140625), -3.140625, 3.140625),
    }


def tables(length, direction):
    indices = jnp.arange(length, dtype=jnp.int32)
    angles = (indices[:, None] * indices[None, :] % length).astype(jnp.float32) * (2.0 * math.pi / length)
    return (jnp.cos(angles).astype(jnp.bfloat16), (direction * jnp.sin(angles)).astype(jnp.bfloat16))

def twiddle(high_len, length, direction):
    row_index = jnp.arange(high_len, dtype=jnp.int32)
    col_index = jnp.arange(LOW, dtype=jnp.int32)
    angles = (row_index[:, None] * col_index[None, :] % length).astype(jnp.float32) * (2.0 * math.pi / length)
    return (jnp.cos(angles), direction * jnp.sin(angles))

def contract(fields, cosine, sine_table, pattern):
    values = fields.astype(jnp.float32)
    first_term = jnp.einsum(pattern, values, cosine.astype(jnp.float32), precision=lax.Precision.HIGHEST)
    second_term = jnp.einsum(pattern, values, sine_table.astype(jnp.float32), precision=lax.Precision.HIGHEST)
    return (first_term[0] - second_term[1], first_term[1] + second_term[0])

def rotate(real_part, imag_part, cosine, sine_table, factor):
    rotated_real = (real_part * cosine - imag_part * sine_table) * factor
    rotated_imag = (imag_part * cosine + real_part * sine_table) * factor
    return jnp.stack([rotated_real, rotated_imag]).astype(jnp.bfloat16)

def transform_pass(fields, prefix, suffix, inverse):
    direction = 1.0 if inverse else -1.0
    dims = fields.shape
    position = fields.ndim - 1 - len(suffix)
    length = dims[position]
    high_len = length // LOW
    split_fields = fields.reshape(dims[:position] + (high_len, LOW) + dims[position + 1:])
    trailing = (1,) * len(suffix)
    high_cos, high_sin = tables(high_len, direction)
    low_cos, low_sin = tables(LOW, direction)
    twist_cos, twist_sin = twiddle(high_len, length, direction)
    twist_cos = twist_cos.reshape((high_len, LOW) + trailing)
    twist_sin = twist_sin.reshape((high_len, LOW) + trailing)
    if inverse:
        real_part, imag_part = contract(split_fields, low_cos, low_sin, prefix + 'km' + suffix + ',ml->' + prefix + 'kl' + suffix)
        middle = rotate(real_part, imag_part, twist_cos, twist_sin, 1.0 / LOW)
        real_part, imag_part = contract(middle, high_cos, high_sin, prefix + 'kl' + suffix + ',kh->' + prefix + 'hl' + suffix)
        factor = 1.0 / high_len
    else:
        real_part, imag_part = contract(split_fields, high_cos, high_sin, prefix + 'hl' + suffix + ',hk->' + prefix + 'kl' + suffix)
        middle = rotate(real_part, imag_part, twist_cos, twist_sin, 1.0)
        real_part, imag_part = contract(middle, low_cos, low_sin, prefix + 'kl' + suffix + ',lm->' + prefix + 'km' + suffix)
        factor = 1.0
    result = jnp.stack([real_part * factor, imag_part * factor]).astype(jnp.bfloat16)
    return result.reshape(dims)

def apply_pupil(fields, phase):
    values = fields.astype(jnp.float32)
    cosine = jnp.cos(phase)
    sine_table = jnp.sin(phase)
    return jnp.stack([values[0] * cosine - values[1] * sine_table, values[0] * sine_table + values[1] * cosine]).astype(jnp.bfloat16)

def pair_terms(fields):
    values = fields.astype(jnp.float32)
    real_part = values[0]
    imag_part = values[1]
    cross_real = lax.optimization_barrier(jnp.sum(real_part[:-1] * real_part[1:] + imag_part[:-1] * imag_part[1:], axis=0))
    cross_imag = lax.optimization_barrier(jnp.sum(imag_part[:-1] * real_part[1:] - real_part[:-1] * imag_part[1:], axis=0))
    power = real_part * real_part + imag_part * imag_part
    energy = 0.5 * lax.optimization_barrier(jnp.sum(power[:-1] + power[1:], axis=0))
    return jnp.stack([cross_real, cross_imag, energy])

def box_sum(padded):
    depth_sum = padded[:, :-2] + padded[:, 1:-1] + padded[:, 2:]
    lateral = depth_sum[:, :, :-2] + depth_sum[:, :, 1:-1] + depth_sum[:, :, 2:]
    return lateral[..., :-2] + lateral[..., 1:-1] + lateral[..., 2:]

def reference(volume, pupil_phase):

    def correct(slice_index):
        fields = lax.dynamic_index_in_dim(volume, slice_index, 1, keepdims=True)
        depth_index = (slice_index % Z).astype(jnp.int32)
        phase = lax.dynamic_index_in_dim(pupil_phase, depth_index, 0, keepdims=True)
        fields = transform_pass(fields, 'cs', 'x', False)
        fields = transform_pass(fields, 'csy', '', False)
        fields = apply_pupil(fields, phase)
        fields = transform_pass(fields, 'csy', '', True)
        fields = transform_pass(fields, 'cs', 'x', True)
        return fields[:, 0]
    corrected = lax.map(correct, jnp.arange(S, dtype=jnp.int32))
    fields = jnp.moveaxis(corrected, 0, 1).reshape(2, R, Z, NY, NX)
    statistics = pair_terms(fields)
    padded = jnp.pad(statistics, ((0, 0), (1, 1), (1, 1), (1, 1)))
    box_sums = box_sum(padded)
    magnitude = jnp.sqrt(box_sums[0] * box_sums[0] + box_sums[1] * box_sums[1])
    return 1.0 - magnitude / (box_sums[2] + 1e-06)
```

```python
import functools

import jax
import jax.numpy as jnp
import ml_dtypes
import numpy as np
from jax import lax
from jax.experimental import pallas as pl
from jax.experimental.pallas import tpu as pltpu
from jax.sharding import PartitionSpec as P


MESH = pl.DeviceIdType.MESH
BF = jnp.bfloat16
F32 = jnp.float32
GX = 16
GY = 32
P0, P1, T0, T2, T3, T5 = 0, 1, 2, 4, 6, 8


def stacked(matrix):
    return np.block([[matrix.real, -matrix.imag], [matrix.imag, matrix.real]])


def constant_tables():
    k4 = np.arange(4)[:, None, None]
    i128 = np.arange(128)
    low = np.exp(-2j * np.pi * (i128[:, None] * i128[None, :] % 128) / 128)
    twist = np.exp(-2j * np.pi * (np.arange(4)[:, None] * i128[None, :] % 512) / 512)
    del k4
    wy = np.stack([stacked(low.T * twist[k][None, :]) for k in range(4)])
    wyi = np.stack([stacked((low.conj() * twist[k].conj()[None, :]).T / 512) for k in range(4)])
    wx = stacked(low).T
    wxi = stacked(low.conj() / 2048).T
    tw = np.exp(-2j * np.pi * (np.arange(16)[:, None] * i128[None, :] % 2048) / 2048)
    bf = ml_dtypes.bfloat16
    return (
        wy.astype(bf),
        wyi.astype(bf),
        np.stack([wx, wxi]).astype(bf),
        np.stack([tw.real, tw.imag]).astype(np.float32),
    )


def dft4(x, q):
    (ar, ai), (br, bi), (cr, ci), (dr, di) = x
    sr, si, tr, ti = ar + cr, ai + ci, ar - cr, ai - ci
    ur, ui, vr, vi = br + dr, bi + di, br - dr, bi - di
    minus = (tr + vi, ti - vr)
    plus = (tr - vi, ti + vr)
    first, third = (minus, plus) if q < 0 else (plus, minus)
    return [(sr + ur, si + ui), first, (sr - ur, si - ui), third]


def dft16(x, q):
    inner = [dft4([x[4 * n + b] for n in range(4)], q) for b in range(4)]
    out = [None] * 16
    for c in range(4):
        column = []
        for b in range(4):
            re, im = inner[b][c]
            if b * c:
                angle = 2 * np.pi * b * c / 16
                wr = float(np.float32(np.cos(angle)).astype(ml_dtypes.bfloat16))
                wi = float(np.float32(q * np.sin(angle)).astype(ml_dtypes.bfloat16))
                if abs(wr) < 1e-6:
                    re, im = (-im, re) if wi > 0 else (im, -re)
                else:
                    re, im = re * wr - im * wi, re * wi + im * wr
            column.append((re, im))
        for d, value in enumerate(dft4(column, q)):
            out[c + 4 * d] = value
    return out


def turn(i, count):
    return lax.rem(i, 2) * ((i + 1) // 2) + (1 - lax.rem(i, 2)) * (count - i // 2)


def kernel(
    vol, pupil, wy_h, wyi_h, wx_h, tw_h, out,
    wy, wyi, wx, tw, ph, ph0, ph1, ph2, cosine, sine,
    buf0, gy_s, send1, buf1, gx_s, cx_s, hx_s, fx_s, send2, buf2, hy_s, stats, send3, buf3,
    ssem, rsem, csem,
):
    a = lax.axis_index("gx")
    g = lax.axis_index("gy")
    z, h = g // 2, lax.rem(g, 2)
    j = 2 * a + h
    lane = lax.broadcasted_iota(jnp.int32, (16, 128), 1)
    low_lane = lane < 64

    loads = [
        pltpu.make_async_copy(s, d, csem.at[n])
        for n, (s, d) in enumerate(
            [(pupil, ph), (wy_h, wy), (wx_h, wx), (tw_h, tw), (wyi_h, wyi)]
        )
    ]
    for copy in loads:
        copy.start()

    barrier = pltpu.get_barrier_semaphore()

    def greet_column(t, _):
        pl.semaphore_signal(
            barrier, inc=1, device_id=(a, lax.rem(g + t, GY)), device_id_type=MESH
        )
        return 0

    def greet_plane(t, _):
        peer = lax.rem(a + t, GX)
        pl.semaphore_signal(barrier, inc=1, device_id=(peer, 2 * z), device_id_type=MESH)
        pl.semaphore_signal(barrier, inc=1, device_id=(peer, 2 * z + 1), device_id_type=MESH)
        return 0

    lax.fori_loop(1, GY, greet_column, 0)
    lax.fori_loop(1, GX, greet_plane, 0)
    loads[0].wait()
    ph0[...] = ph[...].astype(BF)
    pl.semaphore_wait(barrier, 61)

    def remote(src, dst, which, device):
        pltpu.make_async_remote_copy(
            src_ref=src, dst_ref=dst, send_sem=ssem.at[which], recv_sem=rsem.at[which],
            device_id=device, device_id_type=MESH,
        ).start()

    def wait(sem, ref):
        pltpu.make_async_copy(ref, ref, sem).wait()

    def send_p0(t, _):
        zt = lax.rem(z + turn(t, 16), 16)
        remote(ph0.at[zt], ph1.at[z], P0, (a, 2 * zt + h))
        return 0

    lax.fori_loop(1, 16, send_p0, 0)
    pltpu.make_async_copy(ph0.at[z], ph1.at[z], rsem.at[P0]).start()

    for i in range(2):
        def send_t0(t, _, i=i):
            gt = lax.rem(g + turn(t, GY), GY)
            zt, ht = gt // 2, lax.rem(gt, 2)
            remote(vol.at[:, 2 * ht + i, zt], buf0.at[i, :, g], T0 + i, (a, gt))
            return 0

        lax.fori_loop(1, GY, send_t0, 0)
        pltpu.make_async_copy(
            vol.at[:, 2 * h + i, z], buf0.at[i, :, g], rsem.at[T0 + i]
        ).start()

    wait(rsem.at[P0], ph1)

    def send_p1(t, _):
        at = lax.rem(a + turn(t, 16), 16)
        remote(ph1.at[at], ph2.at[a], P1, (at, g))
        return 0

    lax.fori_loop(1, 16, send_p1, 0)
    pltpu.make_async_copy(ph1.at[a], ph2.at[a], rsem.at[P1]).start()
    for copy in loads[1:]:
        copy.wait()
    wait(rsem.at[P1], ph2)

    def angles(k, _):
        phase = ph2[k].astype(F32)
        cosine[k] = jnp.cos(phase)
        sine[k] = jnp.sin(phase)
        return 0

    lax.fori_loop(0, 16, angles, 0)

    def x_stage(i):
        for s in range(2):
            x = [
                (buf1[i, 2 * n + s, 0].astype(F32), buf1[i, 2 * n + s, 1].astype(F32))
                for n in range(16)
            ]
            for k, (re, im) in enumerate(dft16(x, -1)):
                c, w = tw[0, k : k + 1, :], tw[1, k : k + 1, :]
                row = pl.ds(32 * k + 16 * s, 16)
                gx_s[row, 0:128] = (re * c - im * w).astype(BF)
                gx_s[row, 128:256] = (re * w + im * c).astype(BF)
        for b in range(4):
            rows = pl.ds(128 * b, 128)
            f = jnp.dot(gx_s[rows, :], wx[0], preferred_element_type=F32)
            for n in range(8):
                k = 4 * b + n // 2
                re, im = f[16 * n : 16 * n + 16, 0:128], f[16 * n : 16 * n + 16, 128:256]
                row = pl.ds(128 * b + 16 * n, 16)
                cx_s[row, 0:128] = (re * cosine[k] - im * sine[k]).astype(BF)
                cx_s[row, 128:256] = (re * sine[k] + im * cosine[k]).astype(BF)
            hx_s[rows, :] = jnp.dot(cx_s[rows, :], wx[1], preferred_element_type=F32)
        for s in range(2):
            x = []
            for k in range(16):
                c, w = tw[0, k : k + 1, :], tw[1, k : k + 1, :]
                row = pl.ds(32 * k + 16 * s, 16)
                re, im = hx_s[row, 0:128], hx_s[row, 128:256]
                x.append((re * c + im * w, im * c - re * w))
            for n, (re, im) in enumerate(dft16(x, 1)):
                fx_s[s, 0, n] = re
                fx_s[s, 1, n] = im

        def tiles(n, c):
            one, two = fx_s[0, c, n], fx_s[1, c, n]
            turned_one, turned_two = pltpu.roll(one, 64, 1), pltpu.roll(two, 64, 1)
            return one, two, turned_one, turned_two

        at_edge = (lane == 0) | (lane == 63) | (lane == 64) | (lane == 127)
        near = (lane == 0) | (lane == 64)

        def pack(n, _):
            before, after = lax.rem(n + 15, 16), lax.rem(n + 1, 16)
            rims = []
            for c in range(2):
                one, two, turned_one, turned_two = tiles(n, c)
                send2[i, 2 * n, c] = jnp.where(low_lane, one, turned_two).astype(BF)
                send2[i, 2 * n + 1, c] = jnp.where(low_lane, turned_one, two).astype(BF)
                upper = jnp.where(low_lane, turned_two, one)
                lower = jnp.where(low_lane, two, turned_one)
                one, _, _, turned_two = tiles(before, c)
                upper_before = jnp.where(low_lane, turned_two, one)
                _, two, turned_one, _ = tiles(after, c)
                lower_after = jnp.where(low_lane, two, turned_one)
                rims.append(
                    (jnp.where(near, upper, upper_before), jnp.where(near, lower_after, lower))
                )
            for half in range(2):
                send2[i, 2 * n + half, 2] = jnp.where(
                    at_edge, rims[0][half], pltpu.roll(rims[1][half], 2, 1)
                ).astype(BF)
            return 0

        lax.fori_loop(0, 16, pack, 0)

    def plane_device(t):
        jt = lax.rem(j + turn(t, 32), 32)
        return jt, (jt // 2, 2 * z + lax.rem(jt, 2))

    for i in range(2):
        wait(rsem.at[T0 + i], buf0.at[i])

        def columns(n, _, i=i):
            x = [
                (buf0[i, 0, 8 * m + n].astype(F32), buf0[i, 1, 8 * m + n].astype(F32))
                for m in range(4)
            ]
            row = pl.multiple_of(16 * n, 16)
            for k, (re, im) in enumerate(dft4(x, -1)):
                gy_s[k, pl.ds(row, 16), :] = re.astype(BF)
                gy_s[k, pl.ds(128 + row, 16), :] = im.astype(BF)
            return 0

        lax.fori_loop(0, 8, columns, 0)
        for k in range(4):
            f = jnp.dot(wy[k], gy_s[k], preferred_element_type=F32).astype(BF)
            send1[i, 8 * k : 8 * k + 8, 0] = f[0:128].reshape(8, 16, 128)
            send1[i, 8 * k : 8 * k + 8, 1] = f[128:256].reshape(8, 16, 128)

        def send_t2(t, _, i=i):
            jt, device = plane_device(t)
            remote(send1.at[i, jt], buf1.at[i, j], T2 + i, device)
            return 0

        lax.fori_loop(1, 32, send_t2, 0)
        pltpu.make_async_copy(send1.at[i, j], buf1.at[i, j], rsem.at[T2 + i]).start()
        wait(rsem.at[T2 + i], buf1.at[i])

        x_stage(i)

        def send_t3(t, _, i=i):
            jt, device = plane_device(t)
            remote(
                send2.at[i, jt], buf2.at[i, j // 8, :, lax.rem(j, 8)], T3 + i, device
            )
            return 0

        lax.fori_loop(1, 32, send_t3, 0)
        pltpu.make_async_copy(
            send2.at[i, j], buf2.at[i, j // 8, :, lax.rem(j, 8)], rsem.at[T3 + i]
        ).start()
        wait(rsem.at[T3 + i], buf2.at[i])

        for k in range(4):
            main = jnp.concatenate(
                [buf2[i, k, 0].reshape(128, 128), buf2[i, k, 1].reshape(128, 128)], axis=0
            )
            rim = buf2[i, k, 2].reshape(128, 128)
            rim_im = pltpu.roll(rim.astype(F32), 126, 1).astype(BF)
            both = jnp.concatenate([main, jnp.concatenate([rim, rim_im], axis=0)], axis=1)
            hy_s[i, k] = jnp.dot(wyi[k], both, preferred_element_type=F32)

    keep_left = jnp.where((a == 0) & (h == 0), 0.0, 1.0)
    keep_right = jnp.where((a == 15) & (h == 1), 0.0, 1.0)
    rim_mask = jnp.where(lane == 127, keep_left, jnp.where(lane == 64, keep_right, 1.0))
    is_rim = (lane == 127) | (lane == 64)

    stats[:, 0:8, :] = jnp.zeros((3, 8, 128), F32)
    stats[:, 520:528, :] = jnp.zeros((3, 8, 128), F32)

    def pair(ar, ai, br, bi):
        tr, ti = pltpu.roll(ar, 64, 1), pltpu.roll(ai, 64, 1)
        pr, pi = ar * br + ai * bi, ai * br - ar * bi
        u, v = ar * ar + ai * ai, br * br + bi * bi
        return (
            pr + pltpu.roll(pr, 64, 1) + (br * tr + bi * ti),
            pi + pltpu.roll(pi, 64, 1) + (bi * tr - br * ti),
            (0.5 * u + v) + pltpu.roll(u + 0.5 * v, 64, 1),
        )

    def statistics(n, _):
        row = pl.multiple_of(16 * n, 16)
        fields = []
        for part in range(2):
            cols = pl.ds(128 * part, 128)
            pairs = []
            for i in range(2):
                x = [
                    (hy_s[i, k, pl.ds(row, 16), cols], hy_s[i, k, pl.ds(128 + row, 16), cols])
                    for k in range(4)
                ]
                pairs.append(dft4(x, 1))
            fields.append([pair(*pairs[0][m], *pairs[1][m]) for m in range(4)])
        for m in range(4):
            for s in range(3):
                value = jnp.where(is_rim, fields[1][m][s] * rim_mask, fields[0][m][s])
                value = value + pltpu.roll(value, 1, 1) + pltpu.roll(value, 127, 1)
                stats[s, pl.ds(pl.multiple_of(8 + 128 * m + row, 8), 16), :] = value
        return 0

    lax.fori_loop(0, 8, statistics, 0)

    wide_low = lax.broadcasted_iota(jnp.int32, (128, 128), 1) < 64
    for m in range(4):
        sums = []
        for s in range(3):
            base = 8 + 128 * m
            sums.append(
                stats[s, base - 1 : base + 127, :]
                + stats[s, base : base + 128, :]
                + stats[s, base + 1 : base + 129, :]
            )
        cross = jnp.where(wide_low, sums[0], pltpu.roll(sums[1], 64, 1)).astype(BF)
        energy = jnp.where(wide_low, sums[2], pltpu.roll(sums[2], 64, 1)).astype(BF)
        send3[8 * m : 8 * m + 8, 0] = cross.reshape(8, 16, 128)
        send3[8 * m : 8 * m + 8, 1] = energy.reshape(8, 16, 128)

    def send_t5(t, _):
        gt = lax.rem(g + turn(t, GY), GY)
        remote(send3.at[gt], buf3.at[g], T5, (a, gt))
        return 0

    lax.fori_loop(1, GY, send_t5, 0)
    pltpu.make_async_copy(send3.at[g], buf3.at[g], rsem.at[T5]).start()
    wait(rsem.at[T5], buf3)

    def depth(d):
        c0, c1 = buf3[2 * d, 0].astype(F32), buf3[2 * d + 1, 0].astype(F32)
        e = jnp.where(low_lane, buf3[2 * d, 1].astype(F32), buf3[2 * d + 1, 1].astype(F32))
        return c0, c1, e

    window = [None, depth(0), depth(1)]
    for d in range(16):
        present = [w for w in window if w is not None]
        c0, c1, e = [functools.reduce(jnp.add, terms) for terms in zip(*present)]
        s0, s1 = c0 * c0, c1 * c1
        s0, s1 = s0 + pltpu.roll(s0, 64, 1), s1 + pltpu.roll(s1, 64, 1)
        magnitude = jnp.sqrt(jnp.where(low_lane, s0, s1))
        out[d] = 1.0 - magnitude / (e + 1e-6)
        window = window[1:] + [depth(d + 2) if d + 2 < 16 else None]

    wait(ssem.at[P0], ph1.at[0:15])
    wait(ssem.at[P1], ph2.at[0:15])
    for i in range(2):
        wait(ssem.at[T0 + i], buf1.at[i, 0:31])
        wait(ssem.at[T2 + i], buf1.at[i, 0:31])
        wait(ssem.at[T3 + i], send2.at[i, 0:31])
    wait(ssem.at[T5], buf3.at[0:31])


def local(volume, pupil_phase):
    wy, wyi, wx, tw = constant_tables()
    vm = pltpu.VMEM
    return pl.pallas_call(
        kernel,
        out_shape=jax.ShapeDtypeStruct((16, 16, 128), F32),
        in_specs=[pl.BlockSpec(memory_space=pl.ANY)] * 6,
        out_specs=pl.BlockSpec(memory_space=pltpu.VMEM),
        scratch_shapes=[
            vm((4, 256, 256), BF),
            vm((4, 256, 256), BF),
            vm((2, 256, 256), BF),
            vm((2, 16, 128), F32),
            vm((16, 16, 128), F32),
            vm((16, 16, 128), BF),
            vm((16, 16, 128), BF),
            vm((16, 16, 128), BF),
            vm((16, 16, 128), F32),
            vm((16, 16, 128), F32),
            vm((2, 2, 32, 16, 128), BF),
            vm((4, 256, 128), BF),
            vm((2, 32, 2, 16, 128), BF),
            vm((2, 32, 2, 16, 128), BF),
            vm((512, 256), BF),
            vm((512, 256), BF),
            vm((512, 256), F32),
            vm((2, 2, 16, 16, 128), F32),
            vm((2, 32, 3, 16, 128), BF),
            vm((2, 4, 3, 8, 16, 128), BF),
            vm((2, 4, 256, 256), F32),
            vm((3, 528, 128), F32),
            vm((32, 2, 16, 128), BF),
            vm((32, 2, 16, 128), BF),
            pltpu.SemaphoreType.DMA((9,)),
            pltpu.SemaphoreType.DMA((9,)),
            pltpu.SemaphoreType.DMA((5,)),
        ],
        compiler_params=pltpu.CompilerParams(
            collective_id=0, has_side_effects=True, vmem_limit_bytes=40 * 1024 * 1024
        ),
        name="decorrelation",
    )(
        volume.reshape(2, 4, 16, 16, 128),
        pupil_phase,
        jnp.asarray(wy),
        jnp.asarray(wyi),
        jnp.asarray(wx),
        jnp.asarray(tw),
    )


def solution(mesh):
    return jax.shard_map(
        local,
        mesh=mesh,
        in_specs=(P(None, None, "gy", "gx"), P(None, "gy", "gx")),
        out_specs=P(None, "gy", "gx"),
        check_vma=False,
    )
```

```python
import functools

import jax
import jax.numpy as jnp
import ml_dtypes
import numpy as np
from jax import lax
from jax.experimental import pallas as pl
from jax.experimental.pallas import tpu as pltpu
from jax.sharding import PartitionSpec as P


MESH = pl.DeviceIdType.MESH
BF = jnp.bfloat16
F32 = jnp.float32
GX = 16
GY = 32
P0, P1, T0, T2, T3, T5 = 0, 1, 2, 4, 6, 8
EARLY = 16


def stacked(matrix):
    return np.block([[matrix.real, -matrix.imag], [matrix.imag, matrix.real]])


def constant_tables():
    i128 = np.arange(128)
    low = np.exp(-2j * np.pi * (i128[:, None] * i128[None, :] % 128) / 128)
    twist = np.exp(-2j * np.pi * (np.arange(4)[:, None] * i128[None, :] % 512) / 512)
    wy = np.stack([stacked(low.T * twist[k][None, :]) for k in range(4)])
    wyi = np.stack([stacked((low.conj() * twist[k].conj()[None, :]).T / 512) for k in range(4)])
    back = low.conj() / 2048
    wx = np.stack([stacked(m.T).T for m in (low, back, np.roll(back, 64, axis=1))])
    tw = np.exp(-2j * np.pi * (np.arange(16)[:, None] * i128[None, :] % 2048) / 2048)
    turned = np.roll(tw, 64, axis=1)
    bf = ml_dtypes.bfloat16
    return (
        wy.astype(bf),
        wyi.astype(bf),
        wx.astype(bf),
        np.stack([tw.real, tw.imag, turned.real, turned.imag]).astype(np.float32),
    )


def dft4(x, q):
    (ar, ai), (br, bi), (cr, ci), (dr, di) = x
    sr, si, tr, ti = ar + cr, ai + ci, ar - cr, ai - ci
    ur, ui, vr, vi = br + dr, bi + di, br - dr, bi - di
    minus = (tr + vi, ti - vr)
    plus = (tr - vi, ti + vr)
    first, third = (minus, plus) if q < 0 else (plus, minus)
    return [(sr + ur, si + ui), first, (sr - ur, si - ui), third]


def dft16(x, q):
    inner = [dft4([x[4 * n + b] for n in range(4)], q) for b in range(4)]
    out = [None] * 16
    for c in range(4):
        column = []
        for b in range(4):
            re, im = inner[b][c]
            if b * c:
                angle = 2 * np.pi * b * c / 16
                wr = float(np.float32(np.cos(angle)).astype(ml_dtypes.bfloat16))
                wi = float(np.float32(q * np.sin(angle)).astype(ml_dtypes.bfloat16))
                if abs(wr) < 1e-6:
                    re, im = (-im, re) if wi > 0 else (im, -re)
                else:
                    re, im = re * wr - im * wi, re * wi + im * wr
            column.append((re, im))
        for d, value in enumerate(dft4(column, q)):
            out[c + 4 * d] = value
    return out


def turn(i, count):
    return lax.rem(i, 2) * ((i + 1) // 2) + (1 - lax.rem(i, 2)) * (count - i // 2)


def kernel(
    vol, pupil, wy_h, wyi_h, wx_h, tw_h, out,
    wy, wyi, wx, tw, ph, ph0, ph1, ph2, cosine, sine,
    buf0, gy_s, send1, buf1, gx_s, cx_s, hx_s, fx_s, send2, buf2, hy_s, stats, send3, buf3,
    ssem, rsem, csem,
):
    a = lax.axis_index("gx")
    g = lax.axis_index("gy")
    z, h = g // 2, lax.rem(g, 2)
    j = 2 * a + h
    lane = lax.broadcasted_iota(jnp.int32, (16, 128), 1)
    low_lane = lane < 64

    loads = [
        pltpu.make_async_copy(s, d, csem.at[n])
        for n, (s, d) in enumerate(
            [(pupil, ph), (wy_h, wy), (wx_h, wx), (tw_h, tw), (wyi_h, wyi)]
        )
    ]
    for copy in loads:
        copy.start()

    barrier = pltpu.get_barrier_semaphore()

    def greet_column(t, _):
        pl.semaphore_signal(
            barrier, inc=1, device_id=(a, lax.rem(g + t, GY)), device_id_type=MESH
        )
        return 0

    def greet_plane(t, _):
        peer = lax.rem(a + t, GX)
        pl.semaphore_signal(barrier, inc=1, device_id=(peer, 2 * z), device_id_type=MESH)
        pl.semaphore_signal(barrier, inc=1, device_id=(peer, 2 * z + 1), device_id_type=MESH)
        return 0

    lax.fori_loop(1, GY, greet_column, 0)
    lax.fori_loop(1, GX, greet_plane, 0)
    loads[0].wait()
    ph0[...] = ph[...].astype(BF)
    pl.semaphore_wait(barrier, 61)

    def remote(src, dst, which, device):
        pltpu.make_async_remote_copy(
            src_ref=src, dst_ref=dst, send_sem=ssem.at[which], recv_sem=rsem.at[which],
            device_id=device, device_id_type=MESH,
        ).start()

    def wait(sem, ref):
        pltpu.make_async_copy(ref, ref, sem).wait()

    def send_p0(t, _):
        zt = lax.rem(z + turn(t, 16), 16)
        remote(ph0.at[zt], ph1.at[z], P0, (a, 2 * zt + h))
        return 0

    lax.fori_loop(1, 16, send_p0, 0)
    pltpu.make_async_copy(ph0.at[z], ph1.at[z], rsem.at[P0]).start()

    def send_t0(i, first, last):
        def step(t, _):
            gt = lax.rem(g + turn(t, GY), GY)
            zt, ht = gt // 2, lax.rem(gt, 2)
            remote(vol.at[:, 2 * ht + i, zt], buf0.at[i, :, g], T0 + i, (a, gt))
            return 0

        lax.fori_loop(first, last, step, 0)

    def keep_t0(i):
        pltpu.make_async_copy(
            vol.at[:, 2 * h + i, z], buf0.at[i, :, g], rsem.at[T0 + i]
        ).start()

    send_t0(0, 1, GY)
    keep_t0(0)
    keep_t0(1)

    wait(rsem.at[P0], ph1)

    def send_p1(t, _):
        at = lax.rem(a + turn(t, 16), 16)
        remote(ph1.at[at], ph2.at[a], P1, (at, g))
        return 0

    lax.fori_loop(1, 16, send_p1, 0)
    pltpu.make_async_copy(ph1.at[a], ph2.at[a], rsem.at[P1]).start()
    send_t0(1, 1, 1 + EARLY)
    for copy in loads[1:]:
        copy.wait()
    wait(rsem.at[P1], ph2)

    def angles(k, _):
        phase = ph2[k].astype(F32)
        cosine[k] = jnp.cos(phase)
        sine[k] = jnp.sin(phase)
        return 0

    lax.fori_loop(0, 16, angles, 0)

    def y_forward(i):
        def columns(n, _):
            x = [
                (buf0[i, 0, 8 * m + n].astype(F32), buf0[i, 1, 8 * m + n].astype(F32))
                for m in range(4)
            ]
            row = pl.multiple_of(16 * n, 16)
            for k, (re, im) in enumerate(dft4(x, -1)):
                gy_s[k, pl.ds(row, 16), :] = re.astype(BF)
                gy_s[k, pl.ds(128 + row, 16), :] = im.astype(BF)
            return 0

        lax.fori_loop(0, 8, columns, 0)
        for k in range(4):
            f = jnp.dot(wy[k], gy_s[k], preferred_element_type=F32).astype(BF)
            send1[i, 8 * k : 8 * k + 8, 0] = f[0:128].reshape(8, 16, 128)
            send1[i, 8 * k : 8 * k + 8, 1] = f[128:256].reshape(8, 16, 128)

    def send_t2(i):
        def step(t, _):
            jt = lax.rem(j + turn(t, 32), 32)
            remote(send1.at[i, jt], buf1.at[i, j], T2 + i, (jt // 2, 2 * z + lax.rem(jt, 2)))
            return 0

        lax.fori_loop(1, 32, step, 0)
        pltpu.make_async_copy(send1.at[i, j], buf1.at[i, j], rsem.at[T2 + i]).start()

    def x_transforms(i):
        for s in range(2):
            for p in range(2):
                half = slice(8 * p, 8 * p + 8)
                x = [
                    tuple(buf1[i, 2 * n + s, c].astype(F32)[half] for c in range(2))
                    for n in range(16)
                ]
                for k, (re, im) in enumerate(dft16(x, -1)):
                    row = pl.ds(256 * s + 16 * k + 8 * p, 8)
                    c, w = tw[0, k : k + 1, :], tw[1, k : k + 1, :]
                    gx_s[row, 0:128] = re * c - im * w
                    gx_s[row, 128:256] = re * w + im * c
        for s in range(2):
            for b in range(2):
                rows = pl.ds(256 * s + 128 * b, 128)
                f = jnp.dot(gx_s[rows, :].astype(BF), wx[0], preferred_element_type=F32)
                for n in range(8):
                    k = 8 * b + n
                    re, im = f[16 * n : 16 * n + 16, 0:128], f[16 * n : 16 * n + 16, 128:256]
                    row = pl.ds(256 * s + 16 * k, 16)
                    cx_s[row, 0:128] = (re * cosine[k] - im * sine[k]).astype(BF)
                    cx_s[row, 128:256] = (re * sine[k] + im * cosine[k]).astype(BF)
                hx_s[rows, :] = jnp.dot(cx_s[rows, :], wx[1 + s], preferred_element_type=F32)
        for s in range(2):
            for p in range(2):
                x = []
                for k in range(16):
                    row = pl.ds(256 * s + 16 * k + 8 * p, 8)
                    c, w = tw[2 * s, k : k + 1, :], tw[2 * s + 1, k : k + 1, :]
                    re, im = hx_s[row, 0:128], hx_s[row, 128:256]
                    x.append((re * c + im * w, im * c - re * w))
                for n, (re, im) in enumerate(dft16(x, 1)):
                    fx_s[s, 0, n, 8 * p : 8 * p + 8] = re
                    fx_s[s, 1, n, 8 * p : 8 * p + 8] = im

    near = (lane == 0) | (lane == 64)
    at_edge = near | (lane == 63) | (lane == 127)

    def send_t3(i):
        place = buf2.at[i, j // 8, :, lax.rem(j, 8)]

        def straight(n, c):
            return jnp.where(low_lane, fx_s[0, c, n], fx_s[1, c, n])

        def crossed(n, c):
            return jnp.where(low_lane, fx_s[1, c, n], fx_s[0, c, n])

        def pack(n):
            before, after = lax.rem(n + 15, 16), lax.rem(n + 1, 16)
            rims = []
            for c in range(2):
                one, two = straight(n, c), crossed(n, c)
                send2[i, 2 * n, c] = one.astype(BF)
                send2[i, 2 * n + 1, c] = two.astype(BF)
                rims.append(
                    (
                        jnp.where(near, two, crossed(before, c)),
                        jnp.where(near, straight(after, c), one),
                    )
                )
            for half in range(2):
                send2[i, 2 * n + half, 2] = jnp.where(
                    at_edge, rims[0][half], pltpu.roll(rims[1][half], 2, 1)
                ).astype(BF)

        def step(t, _):
            n = lax.rem(a + turn(t, 16), 16)
            pack(n)
            for half in range(2):
                remote(send2.at[i, 2 * n + half], place, T3 + i, (n, 2 * z + half))
            return 0

        lax.fori_loop(1, 16, step, 0)
        pack(a)
        remote(send2.at[i, 2 * a + 1 - h], place, T3 + i, (a, 2 * z + 1 - h))
        pltpu.make_async_copy(send2.at[i, j], place, rsem.at[T3 + i]).start()

    def y_inverse(i):
        for k in range(4):
            main = jnp.concatenate(
                [buf2[i, k, 0].reshape(128, 128), buf2[i, k, 1].reshape(128, 128)], axis=0
            )
            rim = buf2[i, k, 2].reshape(128, 128)
            rim_im = pltpu.roll(rim.astype(F32), 126, 1).astype(BF)
            both = jnp.concatenate([main, jnp.concatenate([rim, rim_im], axis=0)], axis=1)
            hy_s[i, k] = jnp.dot(wyi[k], both, preferred_element_type=F32)

    wait(rsem.at[T0], buf0.at[0])
    y_forward(0)
    send_t2(0)
    send_t0(1, 1 + EARLY, GY)
    wait(rsem.at[T2], buf1.at[0])
    x_transforms(0)
    send_t3(0)
    wait(rsem.at[T0 + 1], buf0.at[1])
    y_forward(1)
    send_t2(1)
    wait(rsem.at[T3], buf2.at[0])
    y_inverse(0)
    wait(rsem.at[T2 + 1], buf1.at[1])
    x_transforms(1)
    send_t3(1)
    wait(rsem.at[T3 + 1], buf2.at[1])
    y_inverse(1)

    left, right = jnp.where(h == 0, 127, 63), jnp.where(h == 0, 64, 0)
    keep_left = jnp.where((a == 0) & (h == 0), 0.0, 1.0)
    keep_right = jnp.where((a == 15) & (h == 1), 0.0, 1.0)
    rim_mask = jnp.where(lane == left, keep_left, keep_right)
    is_rim = (lane == left) | (lane == right)
    own = (lane < 64) == (h == 0)

    stats[:, 0:8, :] = jnp.zeros((3, 8, 128), F32)
    stats[:, 520:528, :] = jnp.zeros((3, 8, 128), F32)

    def pair(ar, ai, br, bi):
        tr, ti = pltpu.roll(ar, 64, 1), pltpu.roll(ai, 64, 1)
        pr, pi = ar * br + ai * bi, ai * br - ar * bi
        u, v = ar * ar + ai * ai, br * br + bi * bi
        real = pr + pltpu.roll(pr, 64, 1) + (br * tr + bi * ti)
        energy = (0.5 * u + v) + pltpu.roll(u + 0.5 * v, 64, 1)
        return energy - real, pi + pltpu.roll(pi, 64, 1) + (bi * tr - br * ti), energy

    def statistics(n):
        row = pl.multiple_of(16 * n, 16)
        fields = []
        for part in range(2):
            cols = pl.ds(128 * part, 128)
            pairs = []
            for i in range(2):
                x = [
                    (hy_s[i, k, pl.ds(row, 16), cols], hy_s[i, k, pl.ds(128 + row, 16), cols])
                    for k in range(4)
                ]
                pairs.append(dft4(x, 1))
            fields.append([pair(*pairs[0][m], *pairs[1][m]) for m in range(4)])
        for m in range(4):
            for s in range(3):
                value = jnp.where(is_rim, fields[1][m][s] * rim_mask, fields[0][m][s])
                value = value + pltpu.roll(value, 1, 1) + pltpu.roll(value, 127, 1)
                stats[s, pl.ds(pl.multiple_of(8 + 128 * m + row, 8), 16), :] = value

    def send_t5(n):
        for m in range(4):
            sums = []
            for s in range(3):
                rows = stats[s, pl.ds(pl.multiple_of(128 * m + 16 * n, 8), 32), :]
                sums.append(rows[7:23] + rows[8:24] + rows[9:25])
            gt = 8 * m + n
            send3[gt, 0] = jnp.where(own, sums[0], pltpu.roll(sums[1], 64, 1)).astype(BF)
            send3[gt, 1] = sums[2].astype(BF)

            @pl.when(gt != g)
            def _():
                remote(send3.at[gt], buf3.at[g], T5, (a, gt))

            @pl.when(gt == g)
            def _():
                pltpu.make_async_copy(send3.at[g], buf3.at[g], rsem.at[T5]).start()

    start = lax.rem(g, 8)

    def first_two(t, _):
        statistics(lax.rem(start + t, 8))
        return 0

    def later(t, _):
        statistics(lax.rem(start + t, 8))
        send_t5(lax.rem(start + t - 1, 8))
        return 0

    def last_two(t, _):
        send_t5(lax.rem(start + t, 8))
        return 0

    lax.fori_loop(0, 2, first_two, 0)
    lax.fori_loop(2, 8, later, 0)
    lax.fori_loop(7, 9, last_two, 0)
    wait(rsem.at[T5], buf3)

    def depth(d):
        c0, c1 = buf3[2 * d, 0].astype(F32), buf3[2 * d + 1, 0].astype(F32)
        e0, e1 = buf3[2 * d, 1].astype(F32), buf3[2 * d + 1, 1].astype(F32)
        return (
            jnp.where(low_lane, c0, c1), jnp.where(low_lane, c1, c0), jnp.where(low_lane, e0, e1)
        )

    window = [None, depth(0), depth(1)]
    for d in range(16):
        present = [w for w in window if w is not None]
        less, imag, energy = [functools.reduce(jnp.add, terms) for terms in zip(*present)]
        real, imag = energy - less, pltpu.roll(imag, 64, 1)
        out[d] = 1.0 - jnp.sqrt(real * real + imag * imag) / (energy + 1e-6)
        window = window[1:] + [depth(d + 2) if d + 2 < 16 else None]

    wait(ssem.at[P0], ph1.at[0:15])
    wait(ssem.at[P1], ph2.at[0:15])
    for i in range(2):
        wait(ssem.at[T0 + i], buf1.at[i, 0:31])
        wait(ssem.at[T2 + i], buf1.at[i, 0:31])
        wait(ssem.at[T3 + i], send2.at[i, 0:31])
    wait(ssem.at[T5], buf3.at[0:31])


def local(volume, pupil_phase):
    wy, wyi, wx, tw = constant_tables()
    vm = pltpu.VMEM
    return pl.pallas_call(
        kernel,
        out_shape=jax.ShapeDtypeStruct((16, 16, 128), F32),
        in_specs=[pl.BlockSpec(memory_space=pltpu.HBM)] * 6,
        out_specs=pl.BlockSpec(memory_space=pltpu.VMEM),
        scratch_shapes=[
            vm((4, 256, 256), BF),
            vm((4, 256, 256), BF),
            vm((3, 256, 256), BF),
            vm((4, 16, 128), F32),
            vm((16, 16, 128), F32),
            vm((16, 16, 128), BF),
            vm((16, 16, 128), BF),
            vm((16, 16, 128), BF),
            vm((16, 16, 128), F32),
            vm((16, 16, 128), F32),
            vm((2, 2, 32, 16, 128), BF),
            vm((4, 256, 128), BF),
            vm((2, 32, 2, 16, 128), BF),
            vm((2, 32, 2, 16, 128), BF),
            vm((512, 256), F32),
            vm((512, 256), BF),
            vm((512, 256), F32),
            vm((2, 2, 16, 16, 128), F32),
            vm((2, 32, 3, 16, 128), BF),
            vm((2, 4, 3, 8, 16, 128), BF),
            vm((2, 4, 256, 256), F32),
            vm((3, 528, 128), F32),
            vm((32, 2, 16, 128), BF),
            vm((32, 2, 16, 128), BF),
            pltpu.SemaphoreType.DMA((9,)),
            pltpu.SemaphoreType.DMA((9,)),
            pltpu.SemaphoreType.DMA((5,)),
        ],
        compiler_params=pltpu.CompilerParams(
            collective_id=0, has_side_effects=True, vmem_limit_bytes=56 * 1024 * 1024
        ),
        name="decorrelation",
    )(
        volume.reshape(2, 4, 16, 16, 128),
        pupil_phase,
        jnp.asarray(wy),
        jnp.asarray(wyi),
        jnp.asarray(wx),
        jnp.asarray(tw),
    )


def solution(mesh):
    return jax.shard_map(
        local,
        mesh=mesh,
        in_specs=(P(None, None, "gy", "gx"), P(None, "gy", "gx")),
        out_specs=P(None, "gy", "gx"),
        check_vma=False,
    )
```

```python
import functools

import jax
import jax.numpy as jnp
import ml_dtypes
import numpy as np
from jax import lax
from jax.experimental import pallas as pl
from jax.experimental.pallas import tpu as pltpu
from jax.sharding import PartitionSpec as P


MESH = pl.DeviceIdType.MESH
BF = jnp.bfloat16
F32 = jnp.float32
GX = 16
GY = 32
P0, P1, T0, T2, T3, T5 = 0, 1, 2, 4, 6, 8
FIRST, SECOND = 16,31


def stacked(matrix):
    return np.block([[matrix.real, -matrix.imag], [matrix.imag, matrix.real]])


def constant_tables():
    i128 = np.arange(128)
    low = np.exp(-2j * np.pi * (i128[:, None] * i128[None, :] % 128) / 128)
    twist = np.exp(-2j * np.pi * (np.arange(4)[:, None] * i128[None, :] % 512) / 512)
    wy = np.stack([stacked(low.T * twist[k][None, :]) for k in range(4)])
    wyi = np.stack([stacked((low.conj() * twist[k].conj()[None, :]).T / 512) for k in range(4)])
    back = low.conj() / 2048
    wx = np.stack([stacked(m.T).T for m in (low, back, np.roll(back, 64, axis=1))])
    tw = np.exp(-2j * np.pi * (np.arange(16)[:, None] * i128[None, :] % 2048) / 2048)
    turned = np.roll(tw, 64, axis=1)
    bf = ml_dtypes.bfloat16
    return (
        wy.astype(bf),
        wyi.astype(bf),
        wx.astype(bf),
        np.stack([tw.real, tw.imag, turned.real, turned.imag]).astype(np.float32),
    )


def dft4(x, q):
    (ar, ai), (br, bi), (cr, ci), (dr, di) = x
    sr, si, tr, ti = ar + cr, ai + ci, ar - cr, ai - ci
    ur, ui, vr, vi = br + dr, bi + di, br - dr, bi - di
    minus = (tr + vi, ti - vr)
    plus = (tr - vi, ti + vr)
    first, third = (minus, plus) if q < 0 else (plus, minus)
    return [(sr + ur, si + ui), first, (sr - ur, si - ui), third]


def dft16(x, q):
    inner = [dft4([x[4 * n + b] for n in range(4)], q) for b in range(4)]
    out = [None] * 16
    for c in range(4):
        column = []
        for b in range(4):
            re, im = inner[b][c]
            if b * c:
                angle = 2 * np.pi * b * c / 16
                wr = float(np.float32(np.cos(angle)).astype(ml_dtypes.bfloat16))
                wi = float(np.float32(q * np.sin(angle)).astype(ml_dtypes.bfloat16))
                if abs(wr) < 1e-6:
                    re, im = (-im, re) if wi > 0 else (im, -re)
                else:
                    re, im = re * wr - im * wi, re * wi + im * wr
            column.append((re, im))
        for d, value in enumerate(dft4(column, q)):
            out[c + 4 * d] = value
    return out


def around(i, step, count):
    moved = i + step
    return jnp.where(moved >= count, moved - count, moved)


STEPS = [s for n in range(1, 8) for s in (n, 16 - n)] + [8]


def kernel(
    vol, pupil, wy_h, wyi_h, wx_h, tw_h, out,
    wy, wyi, wx, tw, ph, ph0, ph1, ph2, cosine, sine,
    buf0, gy_s, send1, buf1, gx_s, cx_s, hx_s, fx_s, send2, buf2, hy_s, stats, send3, buf3,
    ssem, rsem, csem, hand,
):
    a = lax.axis_index("gx")
    g = lax.axis_index("gy")
    z, h = g // 2, lax.rem(g, 2)
    j = 2 * a + h
    lane = lax.broadcasted_iota(jnp.int32, (16, 128), 1)
    low_lane = lane < 64

    loads = [
        pltpu.make_async_copy(s, d, csem.at[n])
        for n, (s, d) in enumerate(
            [(pupil, ph), (wy_h, wy), (wx_h, wx), (tw_h, tw), (wyi_h, wyi)]
        )
    ]
    for copy in loads:
        copy.start()

    barrier = pltpu.get_barrier_semaphore()

    partner = 2 * z + 1 - h
    corners = [a + (1 << b) * (1 - 2 * lax.rem(a // (1 << b), 2)) for b in range(4)]
    greeted = [(a, 2 * around(z, s, 16) + h) for s in STEPS]
    greeted += [(a, partner)] + [(c, g) for c in corners]
    for device in greeted:
        pl.semaphore_signal(barrier, inc=1, device_id=device, device_id_type=MESH)
    loads[0].wait()
    ph0[...] = ph[...].astype(BF)
    pl.semaphore_wait(barrier, 20)

    def pass_on(n, device):
        pl.semaphore_signal(hand.at[n], inc=1, device_id=device, device_id_type=MESH)
        pl.semaphore_wait(hand.at[n], 1)

    def remote(src, dst, which, device):
        pltpu.make_async_remote_copy(
            src_ref=src, dst_ref=dst, send_sem=ssem.at[which], recv_sem=rsem.at[which],
            device_id=device, device_id_type=MESH,
        ).start()

    def wait(sem, ref):
        pltpu.make_async_copy(ref, ref, sem).wait()

    for step in STEPS:
        zt = around(z, step, 16)
        remote(ph0.at[zt], ph1.at[z], P0, (a, 2 * zt + h))
    pltpu.make_async_copy(ph0.at[z], ph1.at[z], rsem.at[P0]).start()

    order = [(s, False) for s in STEPS] + [(s, True) for s in STEPS + [0]]

    def send_t0(i, peers):
        for step, other in peers:
            zt, ht = around(z, step, 16), 1 - h if other else h
            remote(vol.at[:, 2 * ht + i, zt], buf0.at[i, :, g], T0 + i, (a, 2 * zt + ht))

    def keep_t0(i):
        pltpu.make_async_copy(
            vol.at[:, 2 * h + i, z], buf0.at[i, :, g], rsem.at[T0 + i]
        ).start()

    send_t0(0, order[:15])
    pass_on(0, (a, partner))
    send_t0(0, order[15:])
    keep_t0(0)
    send_t0(1, order[:FIRST])
    keep_t0(1)
    for b in range(4):
        pass_on(1 + b, (corners[b], g))

    wait(rsem.at[P0], ph1)

    for step in STEPS:
        at = around(a, step, 16)
        remote(ph1.at[at], ph2.at[a], P1, (at, g))
    pltpu.make_async_copy(ph1.at[a], ph2.at[a], rsem.at[P1]).start()
    for copy in loads[1:]:
        copy.wait()
    wait(rsem.at[P1], ph2)

    def angles(k, _):
        phase = ph2[k].astype(F32)
        cosine[k] = jnp.cos(phase)
        sine[k] = jnp.sin(phase)
        return 0

    lax.fori_loop(0, 16, angles, 0)

    def y_forward(i):
        def columns(n, _):
            x = [
                (buf0[i, 0, 8 * m + n].astype(F32), buf0[i, 1, 8 * m + n].astype(F32))
                for m in range(4)
            ]
            row = pl.multiple_of(16 * n, 16)
            for k, (re, im) in enumerate(dft4(x, -1)):
                gy_s[k, pl.ds(row, 16), :] = re.astype(BF)
                gy_s[k, pl.ds(128 + row, 16), :] = im.astype(BF)
            return 0

        lax.fori_loop(0, 8, columns, 0)
        for k in range(4):
            f = jnp.dot(wy[k], gy_s[k], preferred_element_type=F32).astype(BF)
            send1[i, 8 * k : 8 * k + 8, 0] = f[0:128].reshape(8, 16, 128)
            send1[i, 8 * k : 8 * k + 8, 1] = f[128:256].reshape(8, 16, 128)

    def send_t2(i):
        for step in STEPS + [0]:
            at = around(a, step, 16)
            for ht in (1 - h, h) if step else (1 - h,):
                jt = 2 * at + ht
                remote(send1.at[i, jt], buf1.at[i, j], T2 + i, (at, 2 * z + ht))
        pltpu.make_async_copy(send1.at[i, j], buf1.at[i, j], rsem.at[T2 + i]).start()

    def x_transforms(i):
        for s in range(2):
            for p in range(2):
                half = slice(8 * p, 8 * p + 8)
                x = [
                    tuple(buf1[i, 2 * n + s, c].astype(F32)[half] for c in range(2))
                    for n in range(16)
                ]
                for k, (re, im) in enumerate(dft16(x, -1)):
                    row = pl.ds(256 * s + 16 * k + 8 * p, 8)
                    c, w = tw[0, k : k + 1, :], tw[1, k : k + 1, :]
                    gx_s[row, 0:128] = re * c - im * w
                    gx_s[row, 128:256] = re * w + im * c
        for s in range(2):
            for b in range(2):
                rows = pl.ds(256 * s + 128 * b, 128)
                f = jnp.dot(gx_s[rows, :].astype(BF), wx[0], preferred_element_type=F32)
                for n in range(8):
                    k = 8 * b + n
                    re, im = f[16 * n : 16 * n + 16, 0:128], f[16 * n : 16 * n + 16, 128:256]
                    row = pl.ds(256 * s + 16 * k, 16)
                    cx_s[row, 0:128] = (re * cosine[k] - im * sine[k]).astype(BF)
                    cx_s[row, 128:256] = (re * sine[k] + im * cosine[k]).astype(BF)
                hx_s[rows, :] = jnp.dot(cx_s[rows, :], wx[1 + s], preferred_element_type=F32)
        for s in range(2):
            for p in range(2):
                x = []
                for k in range(16):
                    row = pl.ds(256 * s + 16 * k + 8 * p, 8)
                    c, w = tw[2 * s, k : k + 1, :], tw[2 * s + 1, k : k + 1, :]
                    re, im = hx_s[row, 0:128], hx_s[row, 128:256]
                    x.append((re * c + im * w, im * c - re * w))
                for n, (re, im) in enumerate(dft16(x, 1)):
                    fx_s[s, 0, n, 8 * p : 8 * p + 8] = re
                    fx_s[s, 1, n, 8 * p : 8 * p + 8] = im

    near = (lane == 0) | (lane == 64)
    at_edge = near | (lane == 63) | (lane == 127)

    def send_t3(i):
        place = buf2.at[i, j // 8, :, lax.rem(j, 8)]

        def straight(n, c):
            return jnp.where(low_lane, fx_s[0, c, n], fx_s[1, c, n])

        def crossed(n, c):
            return jnp.where(low_lane, fx_s[1, c, n], fx_s[0, c, n])

        def pack(n):
            before, after = around(n, 15, 16), around(n, 1, 16)
            rims = []
            for c in range(2):
                one, two = straight(n, c), crossed(n, c)
                send2[i, 2 * n, c] = one.astype(BF)
                send2[i, 2 * n + 1, c] = two.astype(BF)
                rims.append(
                    (
                        jnp.where(near, two, crossed(before, c)),
                        jnp.where(near, straight(after, c), one),
                    )
                )
            for half in range(2):
                send2[i, 2 * n + half, 2] = jnp.where(
                    at_edge, rims[0][half], pltpu.roll(rims[1][half], 2, 1)
                ).astype(BF)

        for step in STEPS + [0]:
            n = around(a, step, 16)
            pack(n)
            for ht in (1 - h, h) if step else (1 - h,):
                remote(send2.at[i, 2 * n + ht], place, T3 + i, (n, 2 * z + ht))
        pltpu.make_async_copy(send2.at[i, j], place, rsem.at[T3 + i]).start()

    def y_inverse(i):
        for k in range(4):
            main = jnp.concatenate(
                [buf2[i, k, 0].reshape(128, 128), buf2[i, k, 1].reshape(128, 128)], axis=0
            )
            rim = buf2[i, k, 2].reshape(128, 128)
            rim_im = pltpu.roll(rim.astype(F32), 126, 1).astype(BF)
            both = jnp.concatenate([main, jnp.concatenate([rim, rim_im], axis=0)], axis=1)
            hy_s[i, k] = jnp.dot(wyi[k], both, preferred_element_type=F32)

    wait(rsem.at[T0], buf0.at[0])
    y_forward(0)
    send_t2(0)
    send_t0(1, order[FIRST:SECOND])
    wait(rsem.at[T2], buf1.at[0])
    x_transforms(0)
    send_t3(0)
    send_t0(1, order[SECOND:])
    wait(rsem.at[T0 + 1], buf0.at[1])
    y_forward(1)
    send_t2(1)
    wait(rsem.at[T3], buf2.at[0])
    y_inverse(0)
    wait(rsem.at[T2 + 1], buf1.at[1])
    x_transforms(1)
    send_t3(1)
    wait(rsem.at[T3 + 1], buf2.at[1])
    y_inverse(1)

    left, right = jnp.where(h == 0, 127, 63), jnp.where(h == 0, 64, 0)
    keep_left = jnp.where((a == 0) & (h == 0), 0.0, 1.0)
    keep_right = jnp.where((a == 15) & (h == 1), 0.0, 1.0)
    rim_mask = jnp.where(lane == left, keep_left, keep_right)
    is_rim = (lane == left) | (lane == right)
    own = (lane < 64) == (h == 0)

    stats[:, 0:8, :] = jnp.zeros((3, 8, 128), F32)
    stats[:, 520:528, :] = jnp.zeros((3, 8, 128), F32)

    def pair(ar, ai, br, bi):
        tr, ti = pltpu.roll(ar, 64, 1), pltpu.roll(ai, 64, 1)
        pr, pi = ar * br + ai * bi, ai * br - ar * bi
        u, v = ar * ar + ai * ai, br * br + bi * bi
        real = pr + pltpu.roll(pr, 64, 1) + (br * tr + bi * ti)
        energy = (0.5 * u + v) + pltpu.roll(u + 0.5 * v, 64, 1)
        return energy - real, pi + pltpu.roll(pi, 64, 1) + (bi * tr - br * ti), energy

    def statistics(n):
        row = pl.multiple_of(16 * n, 16)
        fields = []
        for part in range(2):
            cols = pl.ds(128 * part, 128)
            pairs = []
            for i in range(2):
                x = [
                    (hy_s[i, k, pl.ds(row, 16), cols], hy_s[i, k, pl.ds(128 + row, 16), cols])
                    for k in range(4)
                ]
                pairs.append(dft4(x, 1))
            fields.append([pair(*pairs[0][m], *pairs[1][m]) for m in range(4)])
        for m in range(4):
            for s in range(3):
                value = jnp.where(is_rim, fields[1][m][s] * rim_mask, fields[0][m][s])
                value = value + pltpu.roll(value, 1, 1) + pltpu.roll(value, 127, 1)
                stats[s, pl.ds(pl.multiple_of(8 + 128 * m + row, 8), 16), :] = value

    def send_t5(n):
        for m in range(4):
            sums = []
            for s in range(3):
                rows = stats[s, pl.ds(pl.multiple_of(128 * m + 16 * n, 8), 32), :]
                sums.append(rows[7:23] + rows[8:24] + rows[9:25])
            gt = 8 * m + n
            turned = pltpu.roll(sums[2], 64, 1)
            first = jnp.where(h == 0, sums[2], turned)[0:8]
            second = jnp.where(h == 0, turned, sums[2])[8:16]
            send3[gt, 0:16] = jnp.where(own, sums[0], pltpu.roll(sums[1], 64, 1)).astype(BF)
            send3[gt, 16:24] = jnp.where(low_lane[0:8], first, second).astype(BF)

            @pl.when(gt != g)
            def _():
                remote(send3.at[gt], buf3.at[g], T5, (a, gt))

            @pl.when(gt == g)
            def _():
                pltpu.make_async_copy(send3.at[g], buf3.at[g], rsem.at[T5]).start()

    start = lax.rem(g, 8)

    def first_two(t, _):
        statistics(lax.rem(start + t, 8))
        return 0

    def later(t, _):
        statistics(lax.rem(start + t, 8))
        send_t5(lax.rem(start + t - 1, 8))
        return 0

    def last_two(t, _):
        send_t5(lax.rem(start + t, 8))
        return 0

    lax.fori_loop(0, 2, first_two, 0)
    lax.fori_loop(2, 8, later, 0)
    lax.fori_loop(7, 9, last_two, 0)
    wait(rsem.at[T5], buf3)

    def depth(d):
        both = [buf3[2 * d + n].astype(F32) for n in range(2)]
        c0, c1 = both[0][0:16], both[1][0:16]
        e0, e1 = both[0][16:24], both[1][16:24]
        energy = [
            jnp.where(low_lane[0:8], e0, pltpu.roll(e1, 64, 1)),
            jnp.where(low_lane[0:8], pltpu.roll(e0, 64, 1), e1),
        ]
        return (
            jnp.where(low_lane, c0, c1),
            jnp.where(low_lane, c1, c0),
            jnp.concatenate(energy, axis=0),
        )

    window = [None, depth(0), depth(1)]
    for d in range(16):
        present = [w for w in window if w is not None]
        less, imag, energy = [functools.reduce(jnp.add, terms) for terms in zip(*present)]
        real, imag = energy - less, pltpu.roll(imag, 64, 1)
        out[d] = 1.0 - jnp.sqrt(real * real + imag * imag) / (energy + 1e-6)
        window = window[1:] + [depth(d + 2) if d + 2 < 16 else None]

    wait(ssem.at[P0], ph1.at[0:15])
    wait(ssem.at[P1], ph2.at[0:15])
    for i in range(2):
        wait(ssem.at[T0 + i], buf1.at[i, 0:31])
        wait(ssem.at[T2 + i], buf1.at[i, 0:31])
        wait(ssem.at[T3 + i], send2.at[i, 0:31])
    wait(ssem.at[T5], buf3.at[0:31])


def local(volume, pupil_phase):
    wy, wyi, wx, tw = constant_tables()
    vm = pltpu.VMEM
    return pl.pallas_call(
        kernel,
        out_shape=jax.ShapeDtypeStruct((16, 16, 128), F32),
        in_specs=[pl.BlockSpec(memory_space=pltpu.HBM)] * 6,
        out_specs=pl.BlockSpec(memory_space=pltpu.VMEM),
        scratch_shapes=[
            vm((4, 256, 256), BF),
            vm((4, 256, 256), BF),
            vm((3, 256, 256), BF),
            vm((4, 16, 128), F32),
            vm((16, 16, 128), F32),
            vm((16, 16, 128), BF),
            vm((16, 16, 128), BF),
            vm((16, 16, 128), BF),
            vm((16, 16, 128), F32),
            vm((16, 16, 128), F32),
            vm((2, 2, 32, 16, 128), BF),
            vm((4, 256, 128), BF),
            vm((2, 32, 2, 16, 128), BF),
            vm((2, 32, 2, 16, 128), BF),
            vm((512, 256), F32),
            vm((512, 256), BF),
            vm((512, 256), F32),
            vm((2, 2, 16, 16, 128), F32),
            vm((2, 32, 3, 16, 128), BF),
            vm((2, 4, 3, 8, 16, 128), BF),
            vm((2, 4, 256, 256), F32),
            vm((3, 528, 128), F32),
            vm((32, 24, 128), BF),
            vm((32, 24, 128), BF),
            pltpu.SemaphoreType.DMA((9,)),
            pltpu.SemaphoreType.DMA((9,)),
            pltpu.SemaphoreType.DMA((5,)),
            pltpu.SemaphoreType.REGULAR((5,)),
        ],
        compiler_params=pltpu.CompilerParams(
            collective_id=0, has_side_effects=True, vmem_limit_bytes=56 * 1024 * 1024
        ),
        name="decorrelation",
    )(
        volume.reshape(2, 4, 16, 16, 128),
        pupil_phase,
        jnp.asarray(wy),
        jnp.asarray(wyi),
        jnp.asarray(wx),
        jnp.asarray(tw),
    )


def solution(mesh):
    return jax.shard_map(
        local,
        mesh=mesh,
        in_specs=(P(None, None, "gy", "gx"), P(None, "gy", "gx")),
        out_specs=P(None, "gy", "gx"),
        check_vma=False,
    )
```

```python
import functools

import jax
import jax.numpy as jnp
import ml_dtypes
import numpy as np
from jax import lax
from jax.experimental import pallas as pl
from jax.experimental.pallas import tpu as pltpu
from jax.sharding import PartitionSpec as P


MESH = pl.DeviceIdType.MESH
BF = jnp.bfloat16
F32 = jnp.float32
GX = 16
GY = 32
P0, P1, T0, T2, T3, T5 = 0, 1, 2, 4, 6, 8
FIRST, SECOND = 16,31


def stacked(matrix):
    return np.block([[matrix.real, -matrix.imag], [matrix.imag, matrix.real]])


def constant_tables():
    i128 = np.arange(128)
    low = np.exp(-2j * np.pi * (i128[:, None] * i128[None, :] % 128) / 128)
    twist = np.exp(-2j * np.pi * (np.arange(4)[:, None] * i128[None, :] % 512) / 512)
    wy = np.stack([stacked(low.T * twist[k][None, :]) for k in range(4)])
    wyi = np.stack([stacked((low.conj() * twist[k].conj()[None, :]).T / 512) for k in range(4)])
    back = low.conj() / 2048
    wx = np.stack([stacked(m.T).T for m in (low, back, np.roll(back, 64, axis=1))])
    tw = np.exp(-2j * np.pi * (np.arange(16)[:, None] * i128[None, :] % 2048) / 2048)
    turned = np.roll(tw, 64, axis=1)
    bf = ml_dtypes.bfloat16
    return (
        wy.astype(bf),
        wyi.astype(bf),
        wx.astype(bf),
        np.stack([tw.real, tw.imag, turned.real, turned.imag]).astype(np.float32),
    )


def dft4(x, q):
    (ar, ai), (br, bi), (cr, ci), (dr, di) = x
    sr, si, tr, ti = ar + cr, ai + ci, ar - cr, ai - ci
    ur, ui, vr, vi = br + dr, bi + di, br - dr, bi - di
    minus = (tr + vi, ti - vr)
    plus = (tr - vi, ti + vr)
    first, third = (minus, plus) if q < 0 else (plus, minus)
    return [(sr + ur, si + ui), first, (sr - ur, si - ui), third]


def dft16(x, q):
    inner = [dft4([x[4 * n + b] for n in range(4)], q) for b in range(4)]
    out = [None] * 16
    for c in range(4):
        column = []
        for b in range(4):
            re, im = inner[b][c]
            if b * c:
                angle = 2 * np.pi * b * c / 16
                wr = float(np.float32(np.cos(angle)).astype(ml_dtypes.bfloat16))
                wi = float(np.float32(q * np.sin(angle)).astype(ml_dtypes.bfloat16))
                if abs(wr) < 1e-6:
                    re, im = (-im, re) if wi > 0 else (im, -re)
                else:
                    re, im = re * wr - im * wi, re * wi + im * wr
            column.append((re, im))
        for d, value in enumerate(dft4(column, q)):
            out[c + 4 * d] = value
    return out


def around(i, step, count):
    moved = i + step
    return jnp.where(moved >= count, moved - count, moved)


STEPS = [8] + [s for n in range(7, 0, -1) for s in (n, 16 - n)]


def kernel(
    vol, pupil, wy_h, wyi_h, wx_h, tw_h, out,
    wy, wyi, wx, tw, ph, ph0, ph1, ph2, cosine, sine,
    buf0, gy_s, send1, buf1, gx_s, cx_s, hx_s, fx_s, send2, buf2, hy_s, stats, send3, buf3,
    ssem, rsem, csem, hand,
):
    a = lax.axis_index("gx")
    g = lax.axis_index("gy")
    z, h = g // 2, lax.rem(g, 2)
    j = 2 * a + h
    lane = lax.broadcasted_iota(jnp.int32, (16, 128), 1)
    low_lane = lane < 64

    loads = [
        pltpu.make_async_copy(s, d, csem.at[n])
        for n, (s, d) in enumerate(
            [(pupil, ph), (wy_h, wy), (wx_h, wx), (tw_h, tw), (wyi_h, wyi)]
        )
    ]
    for copy in loads:
        copy.start()

    barrier = pltpu.get_barrier_semaphore()

    partner = 2 * z + 1 - h
    corners = [a + (1 << b) * (1 - 2 * lax.rem(a // (1 << b), 2)) for b in range(4)]
    greeted = [(a, 2 * around(z, s, 16) + h) for s in STEPS]
    greeted += [(a, partner)] + [(c, g) for c in corners]
    for device in greeted:
        pl.semaphore_signal(barrier, inc=1, device_id=device, device_id_type=MESH)
    loads[0].wait()
    ph0[...] = ph[...].astype(BF)
    pl.semaphore_wait(barrier, 20)

    def pass_on(n, device):
        pl.semaphore_signal(hand.at[n], inc=1, device_id=device, device_id_type=MESH)
        pl.semaphore_wait(hand.at[n], 1)

    def remote(src, dst, which, device):
        pltpu.make_async_remote_copy(
            src_ref=src, dst_ref=dst, send_sem=ssem.at[which], recv_sem=rsem.at[which],
            device_id=device, device_id_type=MESH,
        ).start()

    def wait(sem, ref):
        pltpu.make_async_copy(ref, ref, sem).wait()

    for step in STEPS:
        zt = around(z, step, 16)
        remote(ph0.at[zt], ph1.at[z], P0, (a, 2 * zt + h))
    pltpu.make_async_copy(ph0.at[z], ph1.at[z], rsem.at[P0]).start()

    order = [(s, False) for s in STEPS] + [(s, True) for s in STEPS + [0]]

    def send_t0(i, peers):
        for step, other in peers:
            zt, ht = around(z, step, 16), 1 - h if other else h
            remote(vol.at[:, 2 * ht + i, zt], buf0.at[i, :, g], T0 + i, (a, 2 * zt + ht))

    def keep_t0(i):
        pltpu.make_async_copy(
            vol.at[:, 2 * h + i, z], buf0.at[i, :, g], rsem.at[T0 + i]
        ).start()

    send_t0(0, order[:15])
    pass_on(0, (a, partner))
    send_t0(0, order[15:])
    keep_t0(0)
    send_t0(1, order[:FIRST])
    keep_t0(1)
    for b in range(4):
        pass_on(1 + b, (corners[b], g))

    wait(rsem.at[P0], ph1)

    for step in STEPS:
        at = around(a, step, 16)
        remote(ph1.at[at], ph2.at[a], P1, (at, g))
    pltpu.make_async_copy(ph1.at[a], ph2.at[a], rsem.at[P1]).start()
    for copy in loads[1:]:
        copy.wait()
    wait(rsem.at[P1], ph2)

    def angles(k, _):
        phase = ph2[k].astype(F32)
        cosine[k] = jnp.cos(phase)
        sine[k] = jnp.sin(phase)
        return 0

    lax.fori_loop(0, 16, angles, 0)

    def y_forward(i):
        def columns(n, _):
            x = [
                (buf0[i, 0, 8 * m + n].astype(F32), buf0[i, 1, 8 * m + n].astype(F32))
                for m in range(4)
            ]
            row = pl.multiple_of(16 * n, 16)
            for k, (re, im) in enumerate(dft4(x, -1)):
                gy_s[k, pl.ds(row, 16), :] = re.astype(BF)
                gy_s[k, pl.ds(128 + row, 16), :] = im.astype(BF)
            return 0

        lax.fori_loop(0, 8, columns, 0)
        for k in range(4):
            f = jnp.dot(wy[k], gy_s[k], preferred_element_type=F32).astype(BF)
            send1[i, 8 * k : 8 * k + 8, 0] = f[0:128].reshape(8, 16, 128)
            send1[i, 8 * k : 8 * k + 8, 1] = f[128:256].reshape(8, 16, 128)

    def send_t2(i):
        for step in STEPS + [0]:
            at = around(a, step, 16)
            for ht in (1 - h, h) if step else (1 - h,):
                jt = 2 * at + ht
                remote(send1.at[i, jt], buf1.at[i, j], T2 + i, (at, 2 * z + ht))
        pltpu.make_async_copy(send1.at[i, j], buf1.at[i, j], rsem.at[T2 + i]).start()

    def x_transforms(i):
        for s in range(2):
            for p in range(2):
                half = slice(8 * p, 8 * p + 8)
                x = [
                    tuple(buf1[i, 2 * n + s, c].astype(F32)[half] for c in range(2))
                    for n in range(16)
                ]
                for k, (re, im) in enumerate(dft16(x, -1)):
                    row = pl.ds(256 * s + 16 * k + 8 * p, 8)
                    c, w = tw[0, k : k + 1, :], tw[1, k : k + 1, :]
                    gx_s[row, 0:128] = re * c - im * w
                    gx_s[row, 128:256] = re * w + im * c
        for s in range(2):
            for b in range(2):
                rows = pl.ds(256 * s + 128 * b, 128)
                f = jnp.dot(gx_s[rows, :].astype(BF), wx[0], preferred_element_type=F32)
                for n in range(8):
                    k = 8 * b + n
                    re, im = f[16 * n : 16 * n + 16, 0:128], f[16 * n : 16 * n + 16, 128:256]
                    row = pl.ds(256 * s + 16 * k, 16)
                    cx_s[row, 0:128] = (re * cosine[k] - im * sine[k]).astype(BF)
                    cx_s[row, 128:256] = (re * sine[k] + im * cosine[k]).astype(BF)
                hx_s[rows, :] = jnp.dot(cx_s[rows, :], wx[1 + s], preferred_element_type=F32)
        for s in range(2):
            for p in range(2):
                x = []
                for k in range(16):
                    row = pl.ds(256 * s + 16 * k + 8 * p, 8)
                    c, w = tw[2 * s, k : k + 1, :], tw[2 * s + 1, k : k + 1, :]
                    re, im = hx_s[row, 0:128], hx_s[row, 128:256]
                    x.append((re * c + im * w, im * c - re * w))
                for n, (re, im) in enumerate(dft16(x, 1)):
                    fx_s[s, 0, n, 8 * p : 8 * p + 8] = re
                    fx_s[s, 1, n, 8 * p : 8 * p + 8] = im

    near = (lane == 0) | (lane == 64)
    at_edge = near | (lane == 63) | (lane == 127)

    def send_t3(i):
        place = buf2.at[i, j // 8, :, lax.rem(j, 8)]

        def straight(n, c):
            return jnp.where(low_lane, fx_s[0, c, n], fx_s[1, c, n])

        def crossed(n, c):
            return jnp.where(low_lane, fx_s[1, c, n], fx_s[0, c, n])

        def pack(n):
            before, after = around(n, 15, 16), around(n, 1, 16)
            rims = []
            for c in range(2):
                one, two = straight(n, c), crossed(n, c)
                send2[i, 2 * n, c] = one.astype(BF)
                send2[i, 2 * n + 1, c] = two.astype(BF)
                rims.append(
                    (
                        jnp.where(near, two, crossed(before, c)),
                        jnp.where(near, straight(after, c), one),
                    )
                )
            for half in range(2):
                send2[i, 2 * n + half, 2] = jnp.where(
                    at_edge, rims[0][half], pltpu.roll(rims[1][half], 2, 1)
                ).astype(BF)

        for step in STEPS + [0]:
            n = around(a, step, 16)
            pack(n)
            for ht in (1 - h, h) if step else (1 - h,):
                remote(send2.at[i, 2 * n + ht], place, T3 + i, (n, 2 * z + ht))
        pltpu.make_async_copy(send2.at[i, j], place, rsem.at[T3 + i]).start()

    def y_inverse(i):
        for k in range(4):
            main = jnp.concatenate(
                [buf2[i, k, 0].reshape(128, 128), buf2[i, k, 1].reshape(128, 128)], axis=0
            )
            rim = buf2[i, k, 2].reshape(128, 128)
            rim_im = pltpu.roll(rim.astype(F32), 126, 1).astype(BF)
            both = jnp.concatenate([main, jnp.concatenate([rim, rim_im], axis=0)], axis=1)
            hy_s[i, k] = jnp.dot(wyi[k], both, preferred_element_type=F32)

    wait(rsem.at[T0], buf0.at[0])
    y_forward(0)
    send_t2(0)
    send_t0(1, order[FIRST:SECOND])
    wait(rsem.at[T2], buf1.at[0])
    x_transforms(0)
    send_t3(0)
    send_t0(1, order[SECOND:])
    wait(rsem.at[T0 + 1], buf0.at[1])
    y_forward(1)
    send_t2(1)
    wait(rsem.at[T3], buf2.at[0])
    y_inverse(0)
    wait(rsem.at[T2 + 1], buf1.at[1])
    x_transforms(1)
    send_t3(1)
    wait(rsem.at[T3 + 1], buf2.at[1])
    y_inverse(1)

    left, right = jnp.where(h == 0, 127, 63), jnp.where(h == 0, 64, 0)
    keep_left = jnp.where((a == 0) & (h == 0), 0.0, 1.0)
    keep_right = jnp.where((a == 15) & (h == 1), 0.0, 1.0)
    rim_mask = jnp.where(lane == left, keep_left, keep_right)
    is_rim = (lane == left) | (lane == right)
    own = (lane < 64) == (h == 0)

    stats[:, 0:8, :] = jnp.zeros((3, 8, 128), F32)
    stats[:, 520:528, :] = jnp.zeros((3, 8, 128), F32)

    def pair(ar, ai, br, bi):
        tr, ti = pltpu.roll(ar, 64, 1), pltpu.roll(ai, 64, 1)
        pr, pi = ar * br + ai * bi, ai * br - ar * bi
        u, v = ar * ar + ai * ai, br * br + bi * bi
        real = pr + pltpu.roll(pr, 64, 1) + (br * tr + bi * ti)
        energy = (0.5 * u + v) + pltpu.roll(u + 0.5 * v, 64, 1)
        return energy - real, pi + pltpu.roll(pi, 64, 1) + (bi * tr - br * ti), energy

    def statistics(n):
        row = pl.multiple_of(16 * n, 16)
        fields = []
        for part in range(2):
            cols = pl.ds(128 * part, 128)
            pairs = []
            for i in range(2):
                x = [
                    (hy_s[i, k, pl.ds(row, 16), cols], hy_s[i, k, pl.ds(128 + row, 16), cols])
                    for k in range(4)
                ]
                pairs.append(dft4(x, 1))
            fields.append([pair(*pairs[0][m], *pairs[1][m]) for m in range(4)])
        for m in range(4):
            for s in range(3):
                value = jnp.where(is_rim, fields[1][m][s] * rim_mask, fields[0][m][s])
                value = value + pltpu.roll(value, 1, 1) + pltpu.roll(value, 127, 1)
                stats[s, pl.ds(pl.multiple_of(8 + 128 * m + row, 8), 16), :] = value

    def send_t5(n):
        for m in range(4):
            sums = []
            for s in range(3):
                rows = stats[s, pl.ds(pl.multiple_of(128 * m + 16 * n, 8), 32), :]
                sums.append(rows[7:23] + rows[8:24] + rows[9:25])
            gt = 8 * m + n
            turned = pltpu.roll(sums[2], 64, 1)
            first = jnp.where(h == 0, sums[2], turned)[0:8]
            second = jnp.where(h == 0, turned, sums[2])[8:16]
            send3[gt, 0:16] = jnp.where(own, sums[0], pltpu.roll(sums[1], 64, 1)).astype(BF)
            send3[gt, 16:24] = jnp.where(low_lane[0:8], first, second).astype(BF)

            @pl.when(gt != g)
            def _():
                remote(send3.at[gt], buf3.at[g], T5, (a, gt))

            @pl.when(gt == g)
            def _():
                pltpu.make_async_copy(send3.at[g], buf3.at[g], rsem.at[T5]).start()

    start = lax.rem(g, 8)

    def first_two(t, _):
        statistics(lax.rem(start + t, 8))
        return 0

    def later(t, _):
        statistics(lax.rem(start + t, 8))
        send_t5(lax.rem(start + t - 1, 8))
        return 0

    def last_two(t, _):
        send_t5(lax.rem(start + t, 8))
        return 0

    lax.fori_loop(0, 2, first_two, 0)
    lax.fori_loop(2, 8, later, 0)
    lax.fori_loop(7, 9, last_two, 0)
    wait(rsem.at[T5], buf3)

    def depth(d):
        both = [buf3[2 * d + n].astype(F32) for n in range(2)]
        c0, c1 = both[0][0:16], both[1][0:16]
        e0, e1 = both[0][16:24], both[1][16:24]
        energy = [
            jnp.where(low_lane[0:8], e0, pltpu.roll(e1, 64, 1)),
            jnp.where(low_lane[0:8], pltpu.roll(e0, 64, 1), e1),
        ]
        return (
            jnp.where(low_lane, c0, c1),
            jnp.where(low_lane, c1, c0),
            jnp.concatenate(energy, axis=0),
        )

    window = [None, depth(0), depth(1)]
    for d in range(16):
        present = [w for w in window if w is not None]
        less, imag, energy = [functools.reduce(jnp.add, terms) for terms in zip(*present)]
        real, imag = energy - less, pltpu.roll(imag, 64, 1)
        out[d] = 1.0 - jnp.sqrt(real * real + imag * imag) / (energy + 1e-6)
        window = window[1:] + [depth(d + 2) if d + 2 < 16 else None]

    wait(ssem.at[P0], ph1.at[0:15])
    wait(ssem.at[P1], ph2.at[0:15])
    for i in range(2):
        wait(ssem.at[T0 + i], buf1.at[i, 0:31])
        wait(ssem.at[T2 + i], buf1.at[i, 0:31])
        wait(ssem.at[T3 + i], send2.at[i, 0:31])
    wait(ssem.at[T5], buf3.at[0:31])


def local(volume, pupil_phase):
    wy, wyi, wx, tw = constant_tables()
    vm = pltpu.VMEM
    return pl.pallas_call(
        kernel,
        out_shape=jax.ShapeDtypeStruct((16, 16, 128), F32),
        in_specs=[pl.BlockSpec(memory_space=pltpu.HBM)] * 6,
        out_specs=pl.BlockSpec(memory_space=pltpu.VMEM),
        scratch_shapes=[
            vm((4, 256, 256), BF),
            vm((4, 256, 256), BF),
            vm((3, 256, 256), BF),
            vm((4, 16, 128), F32),
            vm((16, 16, 128), F32),
            vm((16, 16, 128), BF),
            vm((16, 16, 128), BF),
            vm((16, 16, 128), BF),
            vm((16, 16, 128), F32),
            vm((16, 16, 128), F32),
            vm((2, 2, 32, 16, 128), BF),
            vm((4, 256, 128), BF),
            vm((2, 32, 2, 16, 128), BF),
            vm((2, 32, 2, 16, 128), BF),
            vm((512, 256), F32),
            vm((512, 256), BF),
            vm((512, 256), F32),
            vm((2, 2, 16, 16, 128), F32),
            vm((2, 32, 3, 16, 128), BF),
            vm((2, 4, 3, 8, 16, 128), BF),
            vm((2, 4, 256, 256), F32),
            vm((3, 528, 128), F32),
            vm((32, 24, 128), BF),
            vm((32, 24, 128), BF),
            pltpu.SemaphoreType.DMA((9,)),
            pltpu.SemaphoreType.DMA((9,)),
            pltpu.SemaphoreType.DMA((5,)),
            pltpu.SemaphoreType.REGULAR((5,)),
        ],
        compiler_params=pltpu.CompilerParams(
            collective_id=0, has_side_effects=True, vmem_limit_bytes=56 * 1024 * 1024
        ),
        name="decorrelation",
    )(
        volume.reshape(2, 4, 16, 16, 128),
        pupil_phase,
        jnp.asarray(wy),
        jnp.asarray(wyi),
        jnp.asarray(wx),
        jnp.asarray(tw),
    )


def solution(mesh):
    return jax.shard_map(
        local,
        mesh=mesh,
        in_specs=(P(None, None, "gy", "gx"), P(None, "gy", "gx")),
        out_specs=P(None, "gy", "gx"),
        check_vma=False,
    )
```

```python
import functools

import jax
import jax.numpy as jnp
import ml_dtypes
import numpy as np
from jax import lax
from jax.experimental import pallas as pl
from jax.experimental.pallas import tpu as pltpu
from jax.sharding import PartitionSpec as P


MESH = pl.DeviceIdType.MESH
BF = jnp.bfloat16
F32 = jnp.float32
GX = 16
GY = 32
P0, P1, T0, T2, T3, T5 = 0, 1, 2, 4, 6, 8
FIRST, SECOND = 16,31


def stacked(matrix):
    return np.block([[matrix.real, -matrix.imag], [matrix.imag, matrix.real]])


def constant_tables():
    i128 = np.arange(128)
    low = np.exp(-2j * np.pi * (i128[:, None] * i128[None, :] % 128) / 128)
    twist = np.exp(-2j * np.pi * (np.arange(4)[:, None] * i128[None, :] % 512) / 512)
    wy = np.stack([stacked(low.T * twist[k][None, :]) for k in range(4)])
    wyi = np.stack([stacked((low.conj() * twist[k].conj()[None, :]).T / 512) for k in range(4)])
    back = low.conj() / 2048
    wx = np.stack([stacked(m.T).T for m in (low, back, np.roll(back, 64, axis=1))])
    tw = np.exp(-2j * np.pi * (np.arange(16)[:, None] * i128[None, :] % 2048) / 2048)
    turned = np.roll(tw, 64, axis=1)
    bf = ml_dtypes.bfloat16
    return (
        wy.astype(bf),
        wyi.astype(bf),
        wx.astype(bf),
        np.stack([tw.real, tw.imag, turned.real, turned.imag]).astype(np.float32),
    )


def dft4(x, q):
    (ar, ai), (br, bi), (cr, ci), (dr, di) = x
    sr, si, tr, ti = ar + cr, ai + ci, ar - cr, ai - ci
    ur, ui, vr, vi = br + dr, bi + di, br - dr, bi - di
    minus = (tr + vi, ti - vr)
    plus = (tr - vi, ti + vr)
    first, third = (minus, plus) if q < 0 else (plus, minus)
    return [(sr + ur, si + ui), first, (sr - ur, si - ui), third]


def dft16(x, q):
    inner = [dft4([x[4 * n + b] for n in range(4)], q) for b in range(4)]
    out = [None] * 16
    for c in range(4):
        column = []
        for b in range(4):
            re, im = inner[b][c]
            if b * c:
                angle = 2 * np.pi * b * c / 16
                wr = float(np.float32(np.cos(angle)).astype(ml_dtypes.bfloat16))
                wi = float(np.float32(q * np.sin(angle)).astype(ml_dtypes.bfloat16))
                if abs(wr) < 1e-6:
                    re, im = (-im, re) if wi > 0 else (im, -re)
                else:
                    re, im = re * wr - im * wi, re * wi + im * wr
            column.append((re, im))
        for d, value in enumerate(dft4(column, q)):
            out[c + 4 * d] = value
    return out


def around(i, step, count):
    moved = i + step
    return jnp.where(moved >= count, moved - count, moved)


STEPS = [8] + [s for n in range(7, 0, -1) for s in (n, 16 - n)]


def kernel(
    vol, pupil, wy_h, wyi_h, wx_h, tw_h, out,
    wy, wyi, wx, tw, ph, ph0, ph1, ph2, cosine, sine,
    buf0, gy_s, send1, buf1, gx_s, cx_s, hx_s, fx_s, send2, buf2, hy_s, stats, send3, buf3,
    ssem, rsem, csem, hand,
):
    a = lax.axis_index("gx")
    g = lax.axis_index("gy")
    z, h = g // 2, lax.rem(g, 2)
    j = 2 * a + h
    lane = lax.broadcasted_iota(jnp.int32, (16, 128), 1)
    low_lane = lane < 64

    loads = [
        pltpu.make_async_copy(s, d, csem.at[n])
        for n, (s, d) in enumerate(
            [(pupil, ph), (wy_h, wy), (wx_h, wx), (tw_h, tw), (wyi_h, wyi)]
        )
    ]
    for copy in loads:
        copy.start()

    barrier = pltpu.get_barrier_semaphore()

    partner = 2 * z + 1 - h
    corners = [a + (1 << b) * (1 - 2 * lax.rem(a // (1 << b), 2)) for b in range(4)]
    greeted = [(a, 2 * around(z, s, 16) + h) for s in STEPS]
    greeted += [(a, partner)] + [(c, g) for c in corners]
    for device in greeted:
        pl.semaphore_signal(barrier, inc=1, device_id=device, device_id_type=MESH)
    loads[0].wait()
    ph0[...] = ph[...].astype(BF)
    pl.semaphore_wait(barrier, 20)

    def pass_on(n, device):
        pl.semaphore_signal(hand.at[n], inc=1, device_id=device, device_id_type=MESH)
        pl.semaphore_wait(hand.at[n], 1)

    def remote(src, dst, which, device):
        pltpu.make_async_remote_copy(
            src_ref=src, dst_ref=dst, send_sem=ssem.at[which], recv_sem=rsem.at[which],
            device_id=device, device_id_type=MESH,
        ).start()

    def wait(sem, ref):
        pltpu.make_async_copy(ref, ref, sem).wait()

    for step in STEPS:
        zt = around(z, step, 16)
        remote(ph0.at[zt], ph1.at[z], P0, (a, 2 * zt + h))
    pltpu.make_async_copy(ph0.at[z], ph1.at[z], rsem.at[P0]).start()

    order = [(s, False) for s in STEPS] + [(s, True) for s in STEPS + [0]]

    def send_t0(i, peers):
        for step, other in peers:
            zt, ht = around(z, step, 16), 1 - h if other else h
            remote(vol.at[:, 2 * ht + i, zt], buf0.at[i, :, g], T0 + i, (a, 2 * zt + ht))

    def keep_t0(i):
        pltpu.make_async_copy(
            vol.at[:, 2 * h + i, z], buf0.at[i, :, g], rsem.at[T0 + i]
        ).start()

    send_t0(0, order[:15])
    pass_on(0, (a, partner))
    send_t0(0, order[15:])
    keep_t0(0)
    keep_t0(1)
    for b in range(4):
        pass_on(1 + b, (corners[b], g))

    wait(rsem.at[P0], ph1)

    for step in STEPS:
        at = around(a, step, 16)
        remote(ph1.at[at], ph2.at[a], P1, (at, g))
    pltpu.make_async_copy(ph1.at[a], ph2.at[a], rsem.at[P1]).start()
    send_t0(1, order[:FIRST])
    for copy in loads[1:]:
        copy.wait()

    def angles(k, _):
        phase = ph2[k].astype(F32)
        cosine[k] = jnp.cos(phase)
        sine[k] = jnp.sin(phase)
        return 0

    def y_forward(i):
        def columns(n, _):
            x = [
                (buf0[i, 0, 8 * m + n].astype(F32), buf0[i, 1, 8 * m + n].astype(F32))
                for m in range(4)
            ]
            row = pl.multiple_of(16 * n, 16)
            for k, (re, im) in enumerate(dft4(x, -1)):
                gy_s[k, pl.ds(row, 16), :] = re.astype(BF)
                gy_s[k, pl.ds(128 + row, 16), :] = im.astype(BF)
            return 0

        lax.fori_loop(0, 8, columns, 0)
        for k in range(4):
            f = jnp.dot(wy[k], gy_s[k], preferred_element_type=F32).astype(BF)
            send1[i, 8 * k : 8 * k + 8, 0] = f[0:128].reshape(8, 16, 128)
            send1[i, 8 * k : 8 * k + 8, 1] = f[128:256].reshape(8, 16, 128)

    def send_t2(i):
        for step in STEPS + [0]:
            at = around(a, step, 16)
            for ht in (1 - h, h) if step else (1 - h,):
                jt = 2 * at + ht
                remote(send1.at[i, jt], buf1.at[i, j], T2 + i, (at, 2 * z + ht))
        pltpu.make_async_copy(send1.at[i, j], buf1.at[i, j], rsem.at[T2 + i]).start()

    def x_transforms(i):
        for s in range(2):
            for p in range(2):
                half = slice(8 * p, 8 * p + 8)
                x = [
                    tuple(buf1[i, 2 * n + s, c].astype(F32)[half] for c in range(2))
                    for n in range(16)
                ]
                for k, (re, im) in enumerate(dft16(x, -1)):
                    row = pl.ds(256 * s + 16 * k + 8 * p, 8)
                    c, w = tw[0, k : k + 1, :], tw[1, k : k + 1, :]
                    gx_s[row, 0:128] = re * c - im * w
                    gx_s[row, 128:256] = re * w + im * c
        for s in range(2):
            for b in range(2):
                rows = pl.ds(256 * s + 128 * b, 128)
                f = jnp.dot(gx_s[rows, :].astype(BF), wx[0], preferred_element_type=F32)
                for n in range(8):
                    k = 8 * b + n
                    re, im = f[16 * n : 16 * n + 16, 0:128], f[16 * n : 16 * n + 16, 128:256]
                    row = pl.ds(256 * s + 16 * k, 16)
                    cx_s[row, 0:128] = (re * cosine[k] - im * sine[k]).astype(BF)
                    cx_s[row, 128:256] = (re * sine[k] + im * cosine[k]).astype(BF)
                hx_s[rows, :] = jnp.dot(cx_s[rows, :], wx[1 + s], preferred_element_type=F32)
        for s in range(2):
            for p in range(2):
                x = []
                for k in range(16):
                    row = pl.ds(256 * s + 16 * k + 8 * p, 8)
                    c, w = tw[2 * s, k : k + 1, :], tw[2 * s + 1, k : k + 1, :]
                    re, im = hx_s[row, 0:128], hx_s[row, 128:256]
                    x.append((re * c + im * w, im * c - re * w))
                for n, (re, im) in enumerate(dft16(x, 1)):
                    fx_s[s, 0, n, 8 * p : 8 * p + 8] = re
                    fx_s[s, 1, n, 8 * p : 8 * p + 8] = im

    near = (lane == 0) | (lane == 64)
    at_edge = near | (lane == 63) | (lane == 127)

    def send_t3(i):
        place = buf2.at[i, j // 8, :, lax.rem(j, 8)]

        def straight(n, c):
            return jnp.where(low_lane, fx_s[0, c, n], fx_s[1, c, n])

        def crossed(n, c):
            return jnp.where(low_lane, fx_s[1, c, n], fx_s[0, c, n])

        def pack(n):
            before, after = around(n, 15, 16), around(n, 1, 16)
            rims = []
            for c in range(2):
                one, two = straight(n, c), crossed(n, c)
                send2[i, 2 * n, c] = one.astype(BF)
                send2[i, 2 * n + 1, c] = two.astype(BF)
                rims.append(
                    (
                        jnp.where(near, two, crossed(before, c)),
                        jnp.where(near, straight(after, c), one),
                    )
                )
            for half in range(2):
                send2[i, 2 * n + half, 2] = jnp.where(
                    at_edge, rims[0][half], pltpu.roll(rims[1][half], 2, 1)
                ).astype(BF)

        for step in STEPS + [0]:
            n = around(a, step, 16)
            pack(n)
            for ht in (1 - h, h) if step else (1 - h,):
                remote(send2.at[i, 2 * n + ht], place, T3 + i, (n, 2 * z + ht))
        pltpu.make_async_copy(send2.at[i, j], place, rsem.at[T3 + i]).start()

    def y_inverse(i):
        for k in range(4):
            main = jnp.concatenate(
                [buf2[i, k, 0].reshape(128, 128), buf2[i, k, 1].reshape(128, 128)], axis=0
            )
            rim = buf2[i, k, 2].reshape(128, 128)
            rim_im = pltpu.roll(rim.astype(F32), 126, 1).astype(BF)
            both = jnp.concatenate([main, jnp.concatenate([rim, rim_im], axis=0)], axis=1)
            hy_s[i, k] = jnp.dot(wyi[k], both, preferred_element_type=F32)

    wait(rsem.at[T0], buf0.at[0])
    y_forward(0)
    send_t2(0)
    send_t0(1, order[FIRST:SECOND])
    wait(rsem.at[P1], ph2)
    lax.fori_loop(0, 16, angles, 0)
    wait(rsem.at[T2], buf1.at[0])
    x_transforms(0)
    send_t3(0)
    send_t0(1, order[SECOND:])
    wait(rsem.at[T0 + 1], buf0.at[1])
    y_forward(1)
    send_t2(1)
    wait(rsem.at[T3], buf2.at[0])
    y_inverse(0)
    wait(rsem.at[T2 + 1], buf1.at[1])
    x_transforms(1)
    send_t3(1)
    wait(rsem.at[T3 + 1], buf2.at[1])
    y_inverse(1)

    left, right = jnp.where(h == 0, 127, 63), jnp.where(h == 0, 64, 0)
    keep_left = jnp.where((a == 0) & (h == 0), 0.0, 1.0)
    keep_right = jnp.where((a == 15) & (h == 1), 0.0, 1.0)
    rim_mask = jnp.where(lane == left, keep_left, keep_right)
    is_rim = (lane == left) | (lane == right)
    own = (lane < 64) == (h == 0)

    stats[:, 0:8, :] = jnp.zeros((3, 8, 128), F32)
    stats[:, 520:528, :] = jnp.zeros((3, 8, 128), F32)

    def pair(ar, ai, br, bi):
        tr, ti = pltpu.roll(ar, 64, 1), pltpu.roll(ai, 64, 1)
        pr, pi = ar * br + ai * bi, ai * br - ar * bi
        u, v = ar * ar + ai * ai, br * br + bi * bi
        real = pr + pltpu.roll(pr, 64, 1) + (br * tr + bi * ti)
        energy = (0.5 * u + v) + pltpu.roll(u + 0.5 * v, 64, 1)
        return energy - real, pi + pltpu.roll(pi, 64, 1) + (bi * tr - br * ti), energy

    def statistics(n):
        row = pl.multiple_of(16 * n, 16)
        fields = []
        for part in range(2):
            cols = pl.ds(128 * part, 128)
            pairs = []
            for i in range(2):
                x = [
                    (hy_s[i, k, pl.ds(row, 16), cols], hy_s[i, k, pl.ds(128 + row, 16), cols])
                    for k in range(4)
                ]
                pairs.append(dft4(x, 1))
            fields.append([pair(*pairs[0][m], *pairs[1][m]) for m in range(4)])
        for m in range(4):
            for s in range(3):
                value = jnp.where(is_rim, fields[1][m][s] * rim_mask, fields[0][m][s])
                value = value + pltpu.roll(value, 1, 1) + pltpu.roll(value, 127, 1)
                stats[s, pl.ds(pl.multiple_of(8 + 128 * m + row, 8), 16), :] = value

    FAR, NEAR = (2, 1, 3), (0,)

    def send_t5(n, offsets):
        for offset in offsets:
            m = around(z // 4, offset, 4) if offset else z // 4
            sums = []
            for s in range(3):
                rows = stats[s, pl.ds(pl.multiple_of(128 * m + 16 * n, 8), 32), :]
                sums.append(rows[7:23] + rows[8:24] + rows[9:25])
            gt = 8 * m + n
            turned = pltpu.roll(sums[2], 64, 1)
            first = jnp.where(h == 0, sums[2], turned)[0:8]
            second = jnp.where(h == 0, turned, sums[2])[8:16]
            send3[gt, 0:16] = jnp.where(own, sums[0], pltpu.roll(sums[1], 64, 1)).astype(BF)
            send3[gt, 16:24] = jnp.where(low_lane[0:8], first, second).astype(BF)

            @pl.when(gt != g)
            def _():
                remote(send3.at[gt], buf3.at[g], T5, (a, gt))

            @pl.when(gt == g)
            def _():
                pltpu.make_async_copy(send3.at[g], buf3.at[g], rsem.at[T5]).start()

    start = lax.rem(g, 8)

    def first_two(t, _):
        statistics(lax.rem(start + t, 8))
        return 0

    def later(t, _):
        statistics(lax.rem(start + t, 8))
        send_t5(lax.rem(start + t - 1, 8), FAR)
        return 0

    def last_two(t, _):
        send_t5(lax.rem(start + t, 8), FAR)
        return 0

    def near_ones(t, _):
        send_t5(lax.rem(start + t, 8), NEAR)
        return 0

    lax.fori_loop(0, 2, first_two, 0)
    lax.fori_loop(2, 8, later, 0)
    lax.fori_loop(7, 9, last_two, 0)
    lax.fori_loop(1, 9, near_ones, 0)
    wait(rsem.at[T5], buf3)

    def depth(d):
        both = [buf3[2 * d + n].astype(F32) for n in range(2)]
        c0, c1 = both[0][0:16], both[1][0:16]
        e0, e1 = both[0][16:24], both[1][16:24]
        energy = [
            jnp.where(low_lane[0:8], e0, pltpu.roll(e1, 64, 1)),
            jnp.where(low_lane[0:8], pltpu.roll(e0, 64, 1), e1),
        ]
        return (
            jnp.where(low_lane, c0, c1),
            jnp.where(low_lane, c1, c0),
            jnp.concatenate(energy, axis=0),
        )

    window = [None, depth(0), depth(1)]
    for d in range(16):
        present = [w for w in window if w is not None]
        less, imag, energy = [functools.reduce(jnp.add, terms) for terms in zip(*present)]
        real, imag = energy - less, pltpu.roll(imag, 64, 1)
        out[d] = 1.0 - jnp.sqrt(real * real + imag * imag) / (energy + 1e-6)
        window = window[1:] + [depth(d + 2) if d + 2 < 16 else None]

    wait(ssem.at[P0], ph1.at[0:15])
    wait(ssem.at[P1], ph2.at[0:15])
    for i in range(2):
        wait(ssem.at[T0 + i], buf1.at[i, 0:31])
        wait(ssem.at[T2 + i], buf1.at[i, 0:31])
        wait(ssem.at[T3 + i], send2.at[i, 0:31])
    wait(ssem.at[T5], buf3.at[0:31])


def local(volume, pupil_phase):
    wy, wyi, wx, tw = constant_tables()
    vm = pltpu.VMEM
    return pl.pallas_call(
        kernel,
        out_shape=jax.ShapeDtypeStruct((16, 16, 128), F32),
        in_specs=[pl.BlockSpec(memory_space=pltpu.HBM)] * 6,
        out_specs=pl.BlockSpec(memory_space=pltpu.VMEM),
        scratch_shapes=[
            vm((4, 256, 256), BF),
            vm((4, 256, 256), BF),
            vm((3, 256, 256), BF),
            vm((4, 16, 128), F32),
            vm((16, 16, 128), F32),
            vm((16, 16, 128), BF),
            vm((16, 16, 128), BF),
            vm((16, 16, 128), BF),
            vm((16, 16, 128), F32),
            vm((16, 16, 128), F32),
            vm((2, 2, 32, 16, 128), BF),
            vm((4, 256, 128), BF),
            vm((2, 32, 2, 16, 128), BF),
            vm((2, 32, 2, 16, 128), BF),
            vm((512, 256), F32),
            vm((512, 256), BF),
            vm((512, 256), F32),
            vm((2, 2, 16, 16, 128), F32),
            vm((2, 32, 3, 16, 128), BF),
            vm((2, 4, 3, 8, 16, 128), BF),
            vm((2, 4, 256, 256), F32),
            vm((3, 528, 128), F32),
            vm((32, 24, 128), BF),
            vm((32, 24, 128), BF),
            pltpu.SemaphoreType.DMA((9,)),
            pltpu.SemaphoreType.DMA((9,)),
            pltpu.SemaphoreType.DMA((5,)),
            pltpu.SemaphoreType.REGULAR((5,)),
        ],
        compiler_params=pltpu.CompilerParams(
            collective_id=0, has_side_effects=True, vmem_limit_bytes=56 * 1024 * 1024
        ),
        name="decorrelation",
    )(
        volume.reshape(2, 4, 16, 16, 128),
        pupil_phase,
        jnp.asarray(wy),
        jnp.asarray(wyi),
        jnp.asarray(wx),
        jnp.asarray(tw),
    )


def solution(mesh):
    return jax.shard_map(
        local,
        mesh=mesh,
        in_specs=(P(None, None, "gy", "gx"), P(None, "gy", "gx")),
        out_specs=P(None, "gy", "gx"),
        check_vma=False,
    )
```

```python
import functools

import jax
import jax.numpy as jnp
import ml_dtypes
import numpy as np
from jax import lax
from jax.experimental import pallas as pl
from jax.experimental.pallas import tpu as pltpu
from jax.sharding import PartitionSpec as P


MESH = pl.DeviceIdType.MESH
BF = jnp.bfloat16
F32 = jnp.float32
GX = 16
GY = 32
P0, P1, T0, T2, T3, T5 = 0, 1, 2, 4, 6, 8
FIRST, SECOND = 16,31


def stacked(matrix):
    return np.block([[matrix.real, -matrix.imag], [matrix.imag, matrix.real]])


def constant_tables():
    i128 = np.arange(128)
    low = np.exp(-2j * np.pi * (i128[:, None] * i128[None, :] % 128) / 128)
    twist = np.exp(-2j * np.pi * (np.arange(4)[:, None] * i128[None, :] % 512) / 512)
    wy = np.stack([stacked(low.T * twist[k][None, :]) for k in range(4)])
    wyi = np.stack([stacked((low.conj() * twist[k].conj()[None, :]).T / 512) for k in range(4)])
    back = low.conj() / 2048
    wx = np.stack([stacked(m.T).T for m in (low, back, np.roll(back, 64, axis=1))])
    tw = np.exp(-2j * np.pi * (np.arange(16)[:, None] * i128[None, :] % 2048) / 2048)
    turned = np.roll(tw, 64, axis=1)
    bf = ml_dtypes.bfloat16
    return (
        wy.astype(bf),
        wyi.astype(bf),
        wx.astype(bf),
        np.stack([tw.real, tw.imag, turned.real, turned.imag]).astype(np.float32),
    )


def dft4(x, q):
    (ar, ai), (br, bi), (cr, ci), (dr, di) = x
    sr, si, tr, ti = ar + cr, ai + ci, ar - cr, ai - ci
    ur, ui, vr, vi = br + dr, bi + di, br - dr, bi - di
    minus = (tr + vi, ti - vr)
    plus = (tr - vi, ti + vr)
    first, third = (minus, plus) if q < 0 else (plus, minus)
    return [(sr + ur, si + ui), first, (sr - ur, si - ui), third]


def dft16(x, q):
    inner = [dft4([x[4 * n + b] for n in range(4)], q) for b in range(4)]
    out = [None] * 16
    for c in range(4):
        column = []
        for b in range(4):
            re, im = inner[b][c]
            if b * c:
                angle = 2 * np.pi * b * c / 16
                wr = float(np.float32(np.cos(angle)).astype(ml_dtypes.bfloat16))
                wi = float(np.float32(q * np.sin(angle)).astype(ml_dtypes.bfloat16))
                if abs(wr) < 1e-6:
                    re, im = (-im, re) if wi > 0 else (im, -re)
                else:
                    re, im = re * wr - im * wi, re * wi + im * wr
            column.append((re, im))
        for d, value in enumerate(dft4(column, q)):
            out[c + 4 * d] = value
    return out


def around(i, step, count):
    moved = i + step
    return jnp.where(moved >= count, moved - count, moved)


STEPS = [8] + [s for n in range(7, 0, -1) for s in (n, 16 - n)]


def kernel(
    vol, pupil, wy_h, wyi_h, wx_h, tw_h, out,
    wy, wyi, wx, tw, ph, ph0, ph1, ph2, cosine, sine,
    buf0, gy_s, send1, buf1, gx_s, cx_s, hx_s, fx_s, send2, buf2, hy_s, stats, send3, buf3,
    ssem, rsem, csem, hand, result,
):
    a = lax.axis_index("gx")
    g = lax.axis_index("gy")
    z, h = g // 2, lax.rem(g, 2)
    j = 2 * a + h
    lane = lax.broadcasted_iota(jnp.int32, (16, 128), 1)
    low_lane = lane < 64

    loads = [
        pltpu.make_async_copy(s, d, csem.at[n])
        for n, (s, d) in enumerate(
            [(pupil, ph), (wy_h, wy), (wx_h, wx), (tw_h, tw), (wyi_h, wyi)]
        )
    ]
    for copy in loads:
        copy.start()

    barrier = pltpu.get_barrier_semaphore()

    partner = 2 * z + 1 - h
    corners = [a + (1 << b) * (1 - 2 * lax.rem(a // (1 << b), 2)) for b in range(4)]
    greeted = [(a, 2 * around(z, s, 16) + h) for s in STEPS]
    greeted += [(a, partner)] + [(c, g) for c in corners]
    for device in greeted:
        pl.semaphore_signal(barrier, inc=1, device_id=device, device_id_type=MESH)
    loads[0].wait()
    ph0[...] = ph[...].astype(BF)
    pl.semaphore_wait(barrier, 20)

    def pass_on(n, device):
        pl.semaphore_signal(hand.at[n], inc=1, device_id=device, device_id_type=MESH)
        pl.semaphore_wait(hand.at[n], 1)

    def remote(src, dst, which, device):
        pltpu.make_async_remote_copy(
            src_ref=src, dst_ref=dst, send_sem=ssem.at[which], recv_sem=rsem.at[which],
            device_id=device, device_id_type=MESH,
        ).start()

    def wait(sem, ref):
        pltpu.make_async_copy(ref, ref, sem).wait()

    for step in STEPS:
        zt = around(z, step, 16)
        remote(ph0.at[zt], ph1.at[z], P0, (a, 2 * zt + h))
    pltpu.make_async_copy(ph0.at[z], ph1.at[z], rsem.at[P0]).start()

    order = [(s, False) for s in STEPS] + [(s, True) for s in STEPS + [0]]

    def send_t0(i, peers):
        for step, other in peers:
            zt, ht = around(z, step, 16), 1 - h if other else h
            remote(vol.at[:, 2 * ht + i, zt], buf0.at[i, :, g], T0 + i, (a, 2 * zt + ht))

    def keep_t0(i):
        pltpu.make_async_copy(
            vol.at[:, 2 * h + i, z], buf0.at[i, :, g], rsem.at[T0 + i]
        ).start()

    send_t0(0, order[:15])
    pass_on(0, (a, partner))
    send_t0(0, order[15:])
    keep_t0(0)
    keep_t0(1)
    for b in range(4):
        pass_on(1 + b, (corners[b], g))

    wait(rsem.at[P0], ph1)

    for step in STEPS:
        at = around(a, step, 16)
        remote(ph1.at[at], ph2.at[a], P1, (at, g))
    pltpu.make_async_copy(ph1.at[a], ph2.at[a], rsem.at[P1]).start()
    send_t0(1, order[:FIRST])
    for copy in loads[1:]:
        copy.wait()

    def angles(k, _):
        phase = ph2[k].astype(F32)
        cosine[k] = jnp.cos(phase)
        sine[k] = jnp.sin(phase)
        return 0

    def y_forward(i):
        def columns(n, _):
            x = [
                (buf0[i, 0, 8 * m + n].astype(F32), buf0[i, 1, 8 * m + n].astype(F32))
                for m in range(4)
            ]
            row = pl.multiple_of(16 * n, 16)
            for k, (re, im) in enumerate(dft4(x, -1)):
                gy_s[k, pl.ds(row, 16), :] = re.astype(BF)
                gy_s[k, pl.ds(128 + row, 16), :] = im.astype(BF)
            return 0

        lax.fori_loop(0, 8, columns, 0)
        for k in range(4):
            f = jnp.dot(wy[k], gy_s[k], preferred_element_type=F32).astype(BF)
            send1[i, 8 * k : 8 * k + 8, 0] = f[0:128].reshape(8, 16, 128)
            send1[i, 8 * k : 8 * k + 8, 1] = f[128:256].reshape(8, 16, 128)

    def send_t2(i):
        for step in STEPS + [0]:
            at = around(a, step, 16)
            for ht in (1 - h, h) if step else (1 - h,):
                jt = 2 * at + ht
                remote(send1.at[i, jt], buf1.at[i, j], T2 + i, (at, 2 * z + ht))
        pltpu.make_async_copy(send1.at[i, j], buf1.at[i, j], rsem.at[T2 + i]).start()

    def x_transforms(i):
        for s in range(2):
            for p in range(2):
                half = slice(8 * p, 8 * p + 8)
                x = [
                    tuple(buf1[i, 2 * n + s, c].astype(F32)[half] for c in range(2))
                    for n in range(16)
                ]
                for k, (re, im) in enumerate(dft16(x, -1)):
                    row = pl.ds(256 * s + 16 * k + 8 * p, 8)
                    c, w = tw[0, k : k + 1, :], tw[1, k : k + 1, :]
                    gx_s[row, 0:128] = re * c - im * w
                    gx_s[row, 128:256] = re * w + im * c
        for s in range(2):
            for b in range(2):
                rows = pl.ds(256 * s + 128 * b, 128)
                f = jnp.dot(gx_s[rows, :].astype(BF), wx[0], preferred_element_type=F32)
                for n in range(8):
                    k = 8 * b + n
                    re, im = f[16 * n : 16 * n + 16, 0:128], f[16 * n : 16 * n + 16, 128:256]
                    row = pl.ds(256 * s + 16 * k, 16)
                    cx_s[row, 0:128] = (re * cosine[k] - im * sine[k]).astype(BF)
                    cx_s[row, 128:256] = (re * sine[k] + im * cosine[k]).astype(BF)
                hx_s[rows, :] = jnp.dot(cx_s[rows, :], wx[1 + s], preferred_element_type=F32)
        for s in range(2):
            for p in range(2):
                x = []
                for k in range(16):
                    row = pl.ds(256 * s + 16 * k + 8 * p, 8)
                    c, w = tw[2 * s, k : k + 1, :], tw[2 * s + 1, k : k + 1, :]
                    re, im = hx_s[row, 0:128], hx_s[row, 128:256]
                    x.append((re * c + im * w, im * c - re * w))
                for n, (re, im) in enumerate(dft16(x, 1)):
                    fx_s[s, 0, n, 8 * p : 8 * p + 8] = re
                    fx_s[s, 1, n, 8 * p : 8 * p + 8] = im

    near = (lane == 0) | (lane == 64)
    at_edge = near | (lane == 63) | (lane == 127)

    def send_t3(i):
        place = buf2.at[i, j // 8, :, lax.rem(j, 8)]

        def straight(n, c):
            return jnp.where(low_lane, fx_s[0, c, n], fx_s[1, c, n])

        def crossed(n, c):
            return jnp.where(low_lane, fx_s[1, c, n], fx_s[0, c, n])

        def pack(n):
            before, after = around(n, 15, 16), around(n, 1, 16)
            rims = []
            for c in range(2):
                one, two = straight(n, c), crossed(n, c)
                send2[i, 2 * n, c] = one.astype(BF)
                send2[i, 2 * n + 1, c] = two.astype(BF)
                rims.append(
                    (
                        jnp.where(near, two, crossed(before, c)),
                        jnp.where(near, straight(after, c), one),
                    )
                )
            for half in range(2):
                send2[i, 2 * n + half, 2] = jnp.where(
                    at_edge, rims[0][half], pltpu.roll(rims[1][half], 2, 1)
                ).astype(BF)

        for step in STEPS + [0]:
            n = around(a, step, 16)
            pack(n)
            for ht in (1 - h, h) if step else (1 - h,):
                remote(send2.at[i, 2 * n + ht], place, T3 + i, (n, 2 * z + ht))
        pltpu.make_async_copy(send2.at[i, j], place, rsem.at[T3 + i]).start()

    def y_inverse(i):
        for k in range(4):
            main = jnp.concatenate(
                [buf2[i, k, 0].reshape(128, 128), buf2[i, k, 1].reshape(128, 128)], axis=0
            )
            rim = buf2[i, k, 2].reshape(128, 128)
            rim_im = pltpu.roll(rim.astype(F32), 126, 1).astype(BF)
            both = jnp.concatenate([main, jnp.concatenate([rim, rim_im], axis=0)], axis=1)
            hy_s[i, k] = jnp.dot(wyi[k], both, preferred_element_type=F32)

    wait(rsem.at[T0], buf0.at[0])
    y_forward(0)
    send_t2(0)
    send_t0(1, order[FIRST:SECOND])
    wait(rsem.at[P1], ph2)
    lax.fori_loop(0, 16, angles, 0)
    wait(rsem.at[T2], buf1.at[0])
    x_transforms(0)
    send_t3(0)
    send_t0(1, order[SECOND:])
    wait(rsem.at[T0 + 1], buf0.at[1])
    y_forward(1)
    send_t2(1)
    wait(rsem.at[T2 + 1], buf1.at[1])
    x_transforms(1)
    send_t3(1)
    wait(rsem.at[T3], buf2.at[0])
    y_inverse(0)
    wait(rsem.at[T3 + 1], buf2.at[1])
    y_inverse(1)

    left, right = jnp.where(h == 0, 127, 63), jnp.where(h == 0, 64, 0)
    keep_left = jnp.where((a == 0) & (h == 0), 0.0, 1.0)
    keep_right = jnp.where((a == 15) & (h == 1), 0.0, 1.0)
    rim_mask = jnp.where(lane == left, keep_left, keep_right)
    is_rim = (lane == left) | (lane == right)
    own = (lane < 64) == (h == 0)

    stats[:, 0:8, :] = jnp.zeros((3, 8, 128), F32)
    stats[:, 520:528, :] = jnp.zeros((3, 8, 128), F32)

    def pair(ar, ai, br, bi):
        tr, ti = pltpu.roll(ar, 64, 1), pltpu.roll(ai, 64, 1)
        pr, pi = ar * br + ai * bi, ai * br - ar * bi
        u, v = ar * ar + ai * ai, br * br + bi * bi
        real = pr + pltpu.roll(pr, 64, 1) + (br * tr + bi * ti)
        energy = (0.5 * u + v) + pltpu.roll(u + 0.5 * v, 64, 1)
        return energy - real, pi + pltpu.roll(pi, 64, 1) + (bi * tr - br * ti), energy

    def statistics(n):
        row = pl.multiple_of(16 * n, 16)
        fields = []
        for part in range(2):
            cols = pl.ds(128 * part, 128)
            pairs = []
            for i in range(2):
                x = [
                    (hy_s[i, k, pl.ds(row, 16), cols], hy_s[i, k, pl.ds(128 + row, 16), cols])
                    for k in range(4)
                ]
                pairs.append(dft4(x, 1))
            fields.append([pair(*pairs[0][m], *pairs[1][m]) for m in range(4)])
        for m in range(4):
            for s in range(3):
                value = jnp.where(is_rim, fields[1][m][s] * rim_mask, fields[0][m][s])
                value = value + pltpu.roll(value, 1, 1) + pltpu.roll(value, 127, 1)
                stats[s, pl.ds(pl.multiple_of(8 + 128 * m + row, 8), 16), :] = value

    FAR, NEAR = (2, 1, 3), (0,)

    def send_t5(n, offsets):
        for offset in offsets:
            m = around(z // 4, offset, 4) if offset else z // 4
            sums = []
            for s in range(3):
                rows = stats[s, pl.ds(pl.multiple_of(128 * m + 16 * n, 8), 32), :]
                sums.append(rows[7:23] + rows[8:24] + rows[9:25])
            gt = 8 * m + n
            turned = pltpu.roll(sums[2], 64, 1)
            first = jnp.where(h == 0, sums[2], turned)[0:8]
            second = jnp.where(h == 0, turned, sums[2])[8:16]
            send3[gt, 0:16] = jnp.where(own, sums[0], pltpu.roll(sums[1], 64, 1)).astype(BF)
            send3[gt, 16:24] = jnp.where(low_lane[0:8], first, second).astype(BF)

            @pl.when(gt != g)
            def _():
                remote(send3.at[gt], buf3.at[g], T5, (a, gt))

            @pl.when(gt == g)
            def _():
                pltpu.make_async_copy(send3.at[g], buf3.at[g], rsem.at[T5]).start()

    start = lax.rem(g, 8)

    def first_two(t, _):
        statistics(lax.rem(start + t, 8))
        return 0

    def later(t, _):
        statistics(lax.rem(start + t, 8))
        send_t5(lax.rem(start + t - 1, 8), FAR)
        return 0

    def last_two(t, _):
        send_t5(lax.rem(start + t, 8), FAR)
        return 0

    def near_ones(t, _):
        send_t5(lax.rem(start + t, 8), NEAR)
        return 0

    lax.fori_loop(0, 2, first_two, 0)
    lax.fori_loop(2, 8, later, 0)
    lax.fori_loop(7, 9, last_two, 0)
    lax.fori_loop(1, 9, near_ones, 0)
    wait(rsem.at[T5], buf3)

    def depth(d):
        both = [buf3[2 * d + n].astype(F32) for n in range(2)]
        c0, c1 = both[0][0:16], both[1][0:16]
        e0, e1 = both[0][16:24], both[1][16:24]
        energy = [
            jnp.where(low_lane[0:8], e0, pltpu.roll(e1, 64, 1)),
            jnp.where(low_lane[0:8], pltpu.roll(e0, 64, 1), e1),
        ]
        return (
            jnp.where(low_lane, c0, c1),
            jnp.where(low_lane, c1, c0),
            jnp.concatenate(energy, axis=0),
        )

    stores = []
    window = [None, depth(0), depth(1)]
    for d in range(16):
        present = [w for w in window if w is not None]
        less, imag, energy = [functools.reduce(jnp.add, terms) for terms in zip(*present)]
        real, imag = energy - less, pltpu.roll(imag, 64, 1)
        result[d] = 1.0 - jnp.sqrt(real * real + imag * imag) / (energy + 1e-6)
        window = window[1:] + [depth(d + 2) if d + 2 < 16 else None]
        if d % 4 == 3:
            rows = pl.ds(d - 3, 4)
            stores.append(
                pltpu.make_async_copy(result.at[rows], out.at[rows], csem.at[5 + d // 4])
            )
            stores[-1].start()

    wait(ssem.at[P0], ph1.at[0:15])
    wait(ssem.at[P1], ph2.at[0:15])
    for i in range(2):
        wait(ssem.at[T0 + i], buf1.at[i, 0:31])
        wait(ssem.at[T2 + i], buf1.at[i, 0:31])
        wait(ssem.at[T3 + i], send2.at[i, 0:31])
    wait(ssem.at[T5], buf3.at[0:31])
    for store in stores:
        store.wait()


def local(volume, pupil_phase):
    wy, wyi, wx, tw = constant_tables()
    vm = pltpu.VMEM
    return pl.pallas_call(
        kernel,
        out_shape=jax.ShapeDtypeStruct((16, 16, 128), F32),
        in_specs=[pl.BlockSpec(memory_space=pltpu.HBM)] * 6,
        out_specs=pl.BlockSpec(memory_space=pltpu.HBM),
        scratch_shapes=[
            vm((4, 256, 256), BF),
            vm((4, 256, 256), BF),
            vm((3, 256, 256), BF),
            vm((4, 16, 128), F32),
            vm((16, 16, 128), F32),
            vm((16, 16, 128), BF),
            vm((16, 16, 128), BF),
            vm((16, 16, 128), BF),
            vm((16, 16, 128), F32),
            vm((16, 16, 128), F32),
            vm((2, 2, 32, 16, 128), BF),
            vm((4, 256, 128), BF),
            vm((2, 32, 2, 16, 128), BF),
            vm((2, 32, 2, 16, 128), BF),
            vm((512, 256), F32),
            vm((512, 256), BF),
            vm((512, 256), F32),
            vm((2, 2, 16, 16, 128), F32),
            vm((2, 32, 3, 16, 128), BF),
            vm((2, 4, 3, 8, 16, 128), BF),
            vm((2, 4, 256, 256), F32),
            vm((3, 528, 128), F32),
            vm((32, 24, 128), BF),
            vm((32, 24, 128), BF),
            pltpu.SemaphoreType.DMA((9,)),
            pltpu.SemaphoreType.DMA((9,)),
            pltpu.SemaphoreType.DMA((9,)),
            pltpu.SemaphoreType.REGULAR((5,)),
            vm((16, 16, 128), F32),
        ],
        compiler_params=pltpu.CompilerParams(
            collective_id=0, has_side_effects=True, vmem_limit_bytes=56 * 1024 * 1024
        ),
        name="decorrelation",
    )(
        volume.reshape(2, 4, 16, 16, 128),
        pupil_phase,
        jnp.asarray(wy),
        jnp.asarray(wyi),
        jnp.asarray(wx),
        jnp.asarray(tw),
    )


def solution(mesh):
    return jax.shard_map(
        local,
        mesh=mesh,
        in_specs=(P(None, None, "gy", "gx"), P(None, "gy", "gx")),
        out_specs=P(None, "gy", "gx"),
        check_vma=False,
    )
```
